128 devices in a mesh: sub: 32 (over x, z, core), body: 4 (over y).
Axes of the slice: x: 4, y: 4, z: 4, core: 2. Of those that a mesh axis runs over, the one named last changes fastest.
Arguments:
- compliance: float32 [4, 32, 2400, 2400], P('body', 'sub'), may hold values from -1 to 4, as said below
- mortar: float32 [4, 32, 16, 64, 64], P('body', 'sub'), may hold values from -0.75 to 0.75
- rhs_glue: float32 [4, 32, 176, 128], P('body', 'sub'), may hold values from -6 to 6
- rhs_contact: float32 [4, 32, 16, 64, 128], P('body', 'sub'), may hold values from -6 to 6
- owner_sub: int32 [4, 32, 16, 1], P('body', 'sub'), may hold values from 0 to 31, as said below
- master_slot: int32 [4, 32, 16], P('body', 'sub'), may hold values from 0 to 15
- active_set: int32 [4, 32, 16, 64], P('body', 'sub'), may hold values 0 or 1
Outputs:
- multipliers_glue: float32 [4, 32, 176, 128], P('body', 'sub')
- multipliers_contact: float32 [4, 32, 16, 64, 128], P('body', 'sub')
- residual_glue: float32 [4, 32, 176, 128], P('body', 'sub')
- residual_contact: float32 [4, 32, 16, 64, 128], P('body', 'sub')
The draws below stay inside these ranges and needn't reach their ends.
Inputs may be any that keep to these rules, and one draw needn't show every extreme that they name: `compliance`: symmetric positive definite for every subdomain. `owner_sub`: the master subdomain of a slave segment of subdomain (b, s) is (s + o) mod 32 with o in 0 .. 3. At most 8 slave segments of one subdomain name the same master subdomain, and every subdomain names one master subdomain exactly 8 times.
All inputs are finite; a program needn't handle non-finite values. No bound on the sum of `active_set` on one device may be relied on, other than what follows from the above.
Results may differ from the reference program's by a relative error of at most 0.00015.
Values sent between devices are 32-bit elements; how exact they have to be, the bound alone decides.
No kernel may reach another device: no remote copies, remote signals or barrier semaphores. Data moves between devices by JAX's collectives and lax.ppermute only.
A program may use at most 128 MiB of HBM per device.

```python
import math
import jax
import jax.numpy as jnp
from jax import lax

NS = 2400
SD = 64
SEG = 16
W = 4
CAP = 8
LC = 128
ITERS = 2
G = 176
NSUB = 32
NBODY = 4


def draw_compliance(key, part):
    key = jax.random.fold_in(key, 11)
    first_key, second_key = jax.random.split(key, 2)
    spread = 0.5 / math.sqrt(NS)
    shape = (NBODY, NSUB, NS, NS)
    jitter = jnp.clip(jax.random.normal(first_key, shape, jnp.float32), -4.0, 4.0) * spread
    diagonal = jax.random.uniform(second_key, (NBODY, NSUB, NS), jnp.float32, 1.0, 2.0)
    symmetric = 0.5 * (jitter + jnp.swapaxes(jitter, -1, -2))
    identity = jnp.eye(NS, dtype=jnp.float32)
    return symmetric * (1.0 - identity) + identity * diagonal[..., None]


def draw_owner_sub(key, part):
    key = jax.random.fold_in(key, 5)
    full_key, pick_key, order_key = jax.random.split(key, 3)
    others = (W - 1) * CAP
    full_offset = jax.random.randint(full_key, (NBODY, NSUB, 1), 0, W).astype(jnp.int32)
    other_index = jnp.arange(others, dtype=jnp.int32)
    other_offset = (full_offset + 1 + other_index[None, None, :] // CAP) % W
    pick_scores = jax.random.randint(pick_key, (NBODY, NSUB, others), 0, 1 << 30)
    picked = jnp.argsort(pick_scores, axis=-1, stable=True)[..., :SEG - CAP].astype(jnp.int32)
    chosen = jnp.take_along_axis(other_offset, picked, axis=-1)
    offsets = jnp.concatenate([jnp.broadcast_to(full_offset, (NBODY, NSUB, CAP)), chosen], axis=-1)
    order_scores = jax.random.randint(order_key, (NBODY, NSUB, SEG), 0, 1 << 30)
    order = jnp.argsort(order_scores, axis=-1, stable=True).astype(jnp.int32)
    offsets = jnp.take_along_axis(offsets, order, axis=-1)
    slab = jnp.arange(NSUB, dtype=jnp.int32)[None, :, None]
    owners = (slab + offsets) % NSUB
    return owners[..., None].astype(jnp.int32)


def with_ends(values, key, low, top_value):
    longest = values.shape.index(max(values.shape))
    spots = []
    for shift in (0, 1):
        where = [jax.random.randint(jax.random.fold_in(key, axis), (), 0, length) for axis, length in enumerate(values.shape)]
        where[longest] = (where[longest] + shift) % values.shape[longest]
        spots.append(tuple(where))
    return values.at[spots[0]].set(low).at[spots[1]].set(top_value)


def level_of(rng, dims, cuts, least, top_value):
    def one(axis_at, shards_of):
        draws = jax.random.uniform(jax.random.fold_in(jax.random.fold_in(rng, 6), axis_at), (shards_of,), jnp.float32, least / len(cuts), top_value / len(cuts))
        return jnp.repeat(jnp.exp(draws), dims[axis_at] // shards_of).reshape((-1,) + (1,) * (len(dims) - axis_at - 1))

    loudness = one(*cuts[0])
    for cut in cuts[1:]:
        loudness = loudness * one(*cut)
    return loudness


def normal_values(stream_key, shape, deviation, most, shards=(), kind=jnp.bfloat16):
    entries = deviation * jax.random.normal(stream_key, shape, jnp.float32)
    if shards:
        entries = entries * level_of(stream_key, shape, shards, -0.22, 0.18)
    return jnp.clip(entries, -most, most).astype(kind)


def setup_inputs(seed: int = 0) -> dict:
    seeds = jax.random.split(jax.random.key(seed), 8)
    compliance = draw_compliance(jax.random.fold_in(seeds[7], 71), 0)
    mortar = normal_values(seeds[1], (NBODY, NSUB, SEG, SD, SD), SD ** -0.5, 0.75, ((0, 4), (1, 32)), jnp.float32)
    rhs_glue = normal_values(seeds[2], (NBODY, NSUB, G, LC), 1.0, 6.0, ((0, 4), (1, 32)), jnp.float32)
    rhs_contact = normal_values(seeds[3], (NBODY, NSUB, SEG, SD, LC), 1.0, 6.0, ((0, 4), (1, 32)), jnp.float32)
    owner_sub = draw_owner_sub(jax.random.fold_in(seeds[7], 71), 0)
    master_slot = with_ends(jax.random.randint(seeds[5], (NBODY, NSUB, SEG), 0, SEG), jax.random.fold_in(seeds[5], 1), 0, SEG - 1).astype(jnp.int32)
    active_set = with_ends((jax.random.randint(seeds[6], (NBODY, NSUB, SEG, SD), 0, 4) < 3).astype(jnp.int32), jax.random.fold_in(seeds[6], 1), 0, 1)
    return {"compliance": compliance, "mortar": mortar, "rhs_glue": rhs_glue, "rhs_contact": rhs_contact, "owner_sub": owner_sub, "master_slot": master_slot, "active_set": active_set}


highest = lax.Precision.HIGHEST


def block_product(operands):
    return jnp.dot(operands[0], operands[1], precision=highest)


def dual_apply(compliance, mortar, owner_sub, master_slot, dir_glue, dir_contact):
    body_next = (jnp.arange(NBODY, dtype=jnp.int32) + 1) % NBODY
    target_body = jnp.broadcast_to(body_next[:, None, None], master_slot.shape).astype(jnp.int32)
    target_sub = owner_sub[..., 0].astype(jnp.int32)
    target_slot = master_slot.astype(jnp.int32)
    gathered = jnp.zeros_like(dir_contact).at[target_body, target_sub, target_slot].add(dir_contact)
    master_term = -jnp.einsum("bsjed,bsjel->bsjdl", mortar, gathered, precision=highest)
    left_glue = jnp.concatenate([jnp.zeros_like(dir_glue[:, :1]), dir_glue[:, :-1]], axis=1)
    contact_rows = SEG * SD
    loads = jnp.concatenate([
        -left_glue,
        dir_contact.reshape((NBODY, NSUB, contact_rows, LC)),
        master_term.reshape((NBODY, NSUB, contact_rows, LC)),
        dir_glue], axis=2)
    displaced = lax.map(block_product, (compliance.reshape((NBODY * NSUB, NS, NS)), loads.reshape((NBODY * NSUB, NS, LC))))
    displaced = displaced.reshape((NBODY, NSUB, NS, LC))
    left_face = displaced[:, :, :G]
    slave_part = displaced[:, :, G:G + contact_rows].reshape(dir_contact.shape)
    master_part = displaced[:, :, G + contact_rows:G + 2 * contact_rows].reshape(dir_contact.shape)
    right_face = displaced[:, :, NS - G:]
    next_left = jnp.concatenate([left_face[:, 1:], jnp.zeros_like(left_face[:, :1])], axis=1)
    image_glue = right_face - next_left
    projected = jnp.einsum("bsjde,bsjel->bsjdl", mortar, master_part, precision=highest)
    fetched = projected[target_body, target_sub, target_slot]
    return image_glue, slave_part - fetched


def column_sum(glue_part, contact_part):
    return jnp.sum(glue_part, axis=(0, 1, 2)) + jnp.sum(contact_part, axis=(0, 1, 2, 3))


def reference(compliance, mortar, rhs_glue, rhs_contact, owner_sub, master_slot, active_set):
    mask = active_set.astype(jnp.float32)[..., None]
    res_glue = rhs_glue
    res_contact = rhs_contact * mask
    dir_glue, dir_contact = res_glue, res_contact
    mult_glue = jnp.zeros_like(res_glue)
    mult_contact = jnp.zeros_like(res_contact)
    norm_now = column_sum(res_glue * res_glue, res_contact * res_contact)
    for iteration in range(ITERS):
        image_glue, image_contact = dual_apply(compliance, mortar, owner_sub, master_slot, dir_glue, dir_contact)
        image_contact = image_contact * mask
        curvature = column_sum(dir_glue * image_glue, dir_contact * image_contact)
        alpha = norm_now / curvature
        mult_glue = mult_glue + alpha * dir_glue
        mult_contact = mult_contact + alpha * dir_contact
        res_glue = res_glue - alpha * image_glue
        res_contact = res_contact - alpha * image_contact
        if iteration + 1 < ITERS:
            norm_next = column_sum(res_glue * res_glue, res_contact * res_contact)
            ratio = norm_next / norm_now
            dir_glue = res_glue + ratio * dir_glue
            dir_contact = res_contact + ratio * dir_contact
            norm_now = norm_next
    return mult_glue, mult_contact, res_glue, res_contact
```

```python
import jax
import jax.numpy as jnp
from jax import lax
from jax.experimental import pallas as pl
from jax.experimental.pallas import tpu as pltpu
from jax.sharding import PartitionSpec as P

W = 4
CAP = 8
SLOTS = W * CAP
SEG = 16
SD = 64
LC = 128
G = 176
NS = 2400
CR = SEG * SD
MASTER = G + CR
RIGHT = G + 2 * CR
KP = 2560
K_LOW, K_WIDE = 1152, 1152
TILE = 480
TILES = NS // TILE
INFO = CAP * SD
MIB = 1 << 20

f32 = jnp.float32
bf16 = jnp.bfloat16
highest = lax.Precision.HIGHEST
VM = pl.BlockSpec(memory_space=pltpu.VMEM)
SM = pl.BlockSpec(memory_space=pltpu.SMEM)
ANY = pl.BlockSpec(memory_space=pl.ANY)


def rows(start, size):
    return pl.ds(pl.multiple_of(start, 8), size)


def halves(value):
    high = value.astype(bf16)
    low = (value - high.astype(f32)).astype(bf16)
    return high, low


def product(high, low, both):
    first = jnp.dot(high, both, preferred_element_type=f32)
    second = jnp.dot(low, both, preferred_element_type=f32)
    return (first[:, LC:] + second[:, LC:]) + second[:, :LC] + first[:, :LC]


def pack_kernel(me, owner, slot, act, rhs, out0, out1, out2, out3, pc, mask, source, place, act_wide, count):
    outs = (out0, out1, out2, out3)
    for i in range(SLOTS):
        source[i] = -1
    for o in range(W):
        count[o] = 0
    for k in range(SEG):
        o = lax.rem(owner[k] - me[0] + 32, 32)
        n = count[o]
        source[o * CAP + n] = k
        place[k] = o * CAP + n
        count[o] = n + 1
    active = act[...].astype(f32)
    act_wide[...] = jnp.concatenate([active, jnp.zeros((SEG, 128 - SD), f32)], axis=1)
    columns = jnp.transpose(jnp.concatenate([act_wide[...], jnp.zeros((128 - SEG, 128), f32)], axis=0))
    for k in range(SEG):
        wide = jnp.broadcast_to(columns[:SD, k : k + 1], (SD, LC))
        mask[k * SD : (k + 1) * SD, :] = wide
        pc[k * SD : (k + 1) * SD, :] = rhs[k * SD : (k + 1) * SD, :] * wide
    lane = lax.broadcasted_iota(jnp.int32, (1, 128), 1)
    for o in range(W):
        for n in range(CAP):
            k = source[o * CAP + n]
            at = jnp.maximum(k, 0)
            used = jnp.where(k >= 0, 1.0, 0.0).astype(f32)
            outs[o][n * SD : (n + 1) * SD, :] = pc[rows(at * SD, SD), :] * used
            tag = (slot[at] + 1).astype(f32)
            outs[o][INFO + n : INFO + n + 1, :] = used * jnp.where(lane == SD, tag, act_wide[pl.ds(at, 1), :])


def split_kernel(c_ref, left, pc, pg, high, low, partial, both):
    @pl.when(pl.program_id(0) == 0)
    def _():
        both[...] = jnp.zeros_like(both)
        for start, size, ref, sign in ((0, G, left, -1.0), (G, CR, pc, 1.0), (RIGHT, G, pg, 1.0)):
            part_high, part_low = halves(ref[...] * sign)
            both[start : start + size, :LC] = part_high
            both[start : start + size, LC:] = part_low

    part_high, part_low = halves(c_ref[...])
    pad = jnp.zeros((part_high.shape[0], KP - NS), bf16)
    high[:, :NS] = part_high
    high[:, NS:] = pad
    low[:, :NS] = part_low
    low[:, NS:] = pad
    partial[...] = product(high[...], low[...], both[...])


def start_tiles(high_any, low_any, high, low, sems, first, width):
    copies = []
    for i in range(TILES):
        at = pl.ds(i * TILE, TILE)
        pair = []
        for half, (src, dst) in enumerate(((high_any, high), (low_any, low))):
            copy = pltpu.make_async_copy(src.at[at, pl.ds(first, width)], dst.at[at, :], sems.at[half, i])
            copy.start()
            pair.append(copy)
        copies.append(pair)
    return copies


def mortar_apply(mortar, source, j, transposed):
    block = mortar[j * SD : (j + 1) * SD, :]
    dims = (((0,), (0,)), ((), ())) if transposed else (((1,), (0,)), ((), ()))
    return lax.dot_general(block, source, dims, precision=highest, preferred_element_type=f32)


def column_sum(value):
    return jnp.sum(value, axis=0, keepdims=True)


def first_kernel(
    in0, in1, in2, in3, mortar, left, pc, pg, partial, mask, source, high_any, low_any,
    f0, f1, f2, f3, p0, p1, p2, p3, u, term, projected, actives, slots, sums, left_face, right_face,
    gathered, both, high, low, info, sems, info_sems,
):
    copies = start_tiles(high_any, low_any, high, low, sems, K_LOW, K_WIDE)
    ins = (in0, in1, in2, in3)
    infos = []
    for o in range(W):
        copy = pltpu.make_async_copy(ins[o].at[pl.ds(INFO, 8), :], info.at[pl.ds(o * 8, 8), :], info_sems.at[o])
        copy.start()
        infos.append(copy)
    gathered[...] = jnp.zeros_like(gathered)
    actives[...] = jnp.zeros_like(actives)
    both[...] = jnp.zeros_like(both)
    for copy in infos:
        copy.wait()
    for o in range(W):
        tile = jnp.concatenate([ins[o][INFO : INFO + 8, :], jnp.zeros((120, 128), f32)], axis=0)
        columns = jnp.transpose(tile)
        for n in range(CAP):
            j = info[o * 8 + n, SD].astype(jnp.int32) - 1
            slots[o * CAP + n] = j
            at = rows(jnp.maximum(j, 0) * SD, SD)
            gathered[at, :] += ins[o][n * SD : (n + 1) * SD, :]
            actives[at, :] += jnp.broadcast_to(columns[:SD, n : n + 1], (SD, LC))
    for j in range(SEG):
        value = -mortar_apply(mortar, gathered[j * SD : (j + 1) * SD, :], j, True)
        term[j * SD : (j + 1) * SD, :] = value
        part_high, part_low = halves(value)
        start = MASTER - K_LOW + j * SD
        both[start : start + SD, :LC] = part_high
        both[start : start + SD, LC:] = part_low
    for i in range(TILES):
        at = slice(i * TILE, (i + 1) * TILE)
        for copy in copies[i]:
            copy.wait()
        u[at, :] = partial[at, :] + product(high[at, :], low[at, :], both[...])
    left_face[...] = u[:G, :]
    right_face[...] = u[RIGHT:, :]
    for j in range(SEG):
        start = MASTER + j * SD
        projected[j * SD : (j + 1) * SD, :] = mortar_apply(mortar, u[start : start + SD, :], j, False)
    forward, reply = (f0, f1, f2, f3), (p0, p1, p2, p3)
    for o in range(W):
        for n in range(CAP):
            to = slice(n * SD, (n + 1) * SD)
            k = source[o * CAP + n]
            at = jnp.maximum(k, 0)
            used = jnp.where(k >= 0, 1.0, 0.0).astype(f32)
            forward[o][to, :] = u[rows(G + at * SD, SD), :] * mask[rows(at * SD, SD), :] * used
            j = jnp.maximum(slots[o * CAP + n], 0)
            reply[o][to, :] = projected[rows(j * SD, SD), :]
    norm = column_sum(pg[...] * pg[...]) + column_sum(pc[...] * pc[...])
    curvature = (
        column_sum(pg[...] * u[RIGHT:, :])
        - column_sum(left[...] * u[:G, :])
        + column_sum(pc[...] * u[G:MASTER, :])
        + column_sum(term[...] * u[MASTER:RIGHT, :])
    )
    sums[...] = jnp.concatenate([norm, curvature, jnp.zeros((6, LC), f32)], axis=0)


def second_kernel(
    me, slots, place, f0, f1, f2, f3, b0, b1, b2, b3, next_left, prev_right, u0, projected0, actives, mask,
    mortar, left0, pc, pg, term0, sums0, high_any, low_any,
    p0, p1, p2, p3, u, q_glue, q_contact, sums, left_face,
    gathered, loads, both, high, low, projected, sems,
):
    copies = start_tiles(high_any, low_any, high, low, sems, 0, KP)
    forward, back, reply = (f0, f1, f2, f3), (b0, b1, b2, b3), (p0, p1, p2, p3)
    inner = jnp.where(me[0] > 0, 1.0, 0.0).astype(f32)
    loads[:G, :] = (u0[:G, :] - prev_right[...]) * inner
    glue = u0[RIGHT:, :] - next_left[...]
    q_glue[...] = glue
    loads[RIGHT:, :] = glue
    gathered[...] = -(actives[...] * projected0[...])
    for o in range(W):
        for n in range(CAP):
            at = rows(jnp.maximum(slots[o * CAP + n], 0) * SD, SD)
            gathered[at, :] += forward[o][n * SD : (n + 1) * SD, :]
    for k in range(SEG):
        seat = place[k]
        o, n = lax.div(seat, CAP), lax.rem(seat, CAP)
        here = slice(k * SD, (k + 1) * SD)
        fetched = jnp.zeros((SD, LC), f32)
        for w in range(W):
            fetched = jnp.where(o == w, back[w][rows(n * SD, SD), :], fetched)
        value = mask[here, :] * (u0[G + k * SD : G + (k + 1) * SD, :] - fetched)
        q_contact[here, :] = value
        loads[G + k * SD : G + (k + 1) * SD, :] = value
    for j in range(SEG):
        value = -mortar_apply(mortar, gathered[j * SD : (j + 1) * SD, :], j, True)
        loads[MASTER + j * SD : MASTER + (j + 1) * SD, :] = value
    part_high, part_low = halves(loads[...])
    both[:NS, :LC] = part_high
    both[:NS, LC:] = part_low
    both[NS:, :] = jnp.zeros((KP - NS, 2 * LC), bf16)
    for i in range(TILES):
        at = slice(i * TILE, (i + 1) * TILE)
        for copy in copies[i]:
            copy.wait()
        u[at, :] = product(high[at, :], low[at, :], both[...])
    left_face[...] = u[:G, :]
    for j in range(SEG):
        start = MASTER + j * SD
        projected[j * SD : (j + 1) * SD, :] = mortar_apply(mortar, u[start : start + SD, :], j, False)
    for o in range(W):
        for n in range(CAP):
            j = jnp.maximum(slots[o * CAP + n], 0)
            reply[o][n * SD : (n + 1) * SD, :] = projected[rows(j * SD, SD), :]
    alpha = sums0[0:1, :] / sums0[1:2, :]
    res_glue = pg[...] - alpha * q_glue[...]
    res_contact = pc[...] - alpha * q_contact[...]
    norm = column_sum(res_glue * res_glue) + column_sum(res_contact * res_contact)
    own = jnp.zeros((1, LC), f32)
    cross = jnp.zeros((1, LC), f32)
    for start, size, first, sign in ((0, G, left0, -1.0), (G, CR, pc, 1.0), (MASTER, CR, term0, 1.0), (RIGHT, G, pg, 1.0)):
        at = slice(start, start + size)
        load = first[...] * sign - alpha * loads[at, :]
        own = own + column_sum(load * (u0[at, :] - alpha * u[at, :]))
        cross = cross + column_sum(load * u0[at, :])
    sums[...] = jnp.concatenate([norm, own, cross, jnp.zeros((5, LC), f32)], axis=0)


def last_kernel(
    place, b0, b1, b2, b3, next_left, u, q_glue, q_contact, pc, pg, mask, sums0, sums1,
    mult_glue, mult_contact, res_glue, res_contact,
):
    back = (b0, b1, b2, b3)
    norm0, curvature0 = sums0[0:1, :], sums0[1:2, :]
    norm1, own, cross = sums1[0:1, :], sums1[1:2, :], sums1[2:3, :]
    alpha0 = norm0 / curvature0
    ratio = norm1 / norm0
    curvature1 = own + ratio * (2.0 * cross + ratio * curvature0)
    alpha1 = norm1 / curvature1

    def finish(r0, q, w):
        r1 = r0 - alpha0 * q
        direction = r1 + ratio * r0
        image = (q - alpha0 * w) + ratio * q
        return alpha0 * r0 + alpha1 * direction, r1 - alpha1 * image

    mult, res = finish(pg[...], q_glue[...], u[RIGHT:, :] - next_left[...])
    mult_glue[...] = mult
    res_glue[...] = res
    for k in range(SEG):
        seat = place[k]
        o, n = lax.div(seat, CAP), lax.rem(seat, CAP)
        here = slice(k * SD, (k + 1) * SD)
        fetched = jnp.zeros((SD, LC), f32)
        for w in range(W):
            fetched = jnp.where(o == w, back[w][rows(n * SD, SD), :], fetched)
        value = mask[here, :] * (u[G + k * SD : G + (k + 1) * SD, :] - fetched)
        mult, res = finish(pc[here, :], q_contact[here, :], value)
        mult_contact[here, :] = mult
        res_contact[here, :] = res


def shape(*dims, dtype=f32):
    return jax.ShapeDtypeStruct(dims, dtype)


def params(mib):
    return pltpu.CompilerParams(vmem_limit_bytes=mib * MIB)


def sent(value, body_step, sub_step):
    subs, bodies = lax.axis_size("sub"), lax.axis_size("body")
    pairs = [
        (s * bodies + b, ((s + sub_step) % subs) * bodies + (b + body_step) % bodies)
        for s in range(subs)
        for b in range(bodies)
    ]
    return lax.ppermute(value, ("sub", "body"), pairs)


def passed_along(value, steps):
    count = lax.axis_size("sub")
    first, last = (max(0, -steps), min(count, count - steps))
    return lax.ppermute(value, "sub", [(source, source + steps) for source in range(first, last)])


def rotated(value, block, stride, steps):
    count = lax.axis_size("sub")
    pairs = []
    for s in range(count):
        place = s // stride % block
        pairs.append((s, s + ((place + steps) % block - place) * stride))
    return lax.ppermute(value, "sub", pairs)


def total(value):
    value = value + sent(value, 1, 0) + sent(value, 2, 0) + sent(value, 3, 0)
    for stride in (8, 2):
        value = value + sum(rotated(value, 4, stride, k) for k in (1, 2, 3))
    return value + rotated(value, 2, 1, 1)


def per_device(compliance, mortar, rhs_glue, rhs_contact, owner_sub, master_slot, active_set):
    schur_block = compliance[0, 0]
    blocks = mortar.reshape(CR, SD)
    pg = rhs_glue[0, 0]
    rhs = rhs_contact.reshape(CR, LC)
    me = lax.axis_index("sub").astype(jnp.int32).reshape(1)
    seg_block = shape(INFO, LC)

    *outgoing, pc, mask, source, place = pl.pallas_call(
        pack_kernel,
        out_shape=[shape(INFO + 8, LC)] * 4
        + [shape(CR, LC)] * 2
        + [shape(SLOTS, dtype=jnp.int32), shape(SEG, dtype=jnp.int32)],
        in_specs=[SM, SM, SM, VM, VM],
        out_specs=[VM] * 6 + [SM] * 2,
        scratch_shapes=[pltpu.VMEM((SEG, 128), f32), pltpu.SMEM((W,), jnp.int32)],
        compiler_params=params(16),
        name="pack",
    )(me, owner_sub.reshape(SEG), master_slot.reshape(SEG), active_set.reshape(SEG, SD), rhs)

    incoming = [sent(outgoing[o], 1, o) for o in range(W)]
    left = passed_along(pg, 1)

    block_rows = 240
    steps = NS // block_rows
    high, low, partial = pl.pallas_call(
        split_kernel,
        grid=(steps,),
        out_shape=[shape(NS, KP, dtype=bf16)] * 2 + [shape(NS, LC)],
        in_specs=[
            pl.BlockSpec((block_rows, NS), lambda i: (i, 0)),
            pl.BlockSpec((G, LC), lambda i: (0, 0)),
            pl.BlockSpec((CR, LC), lambda i: (0, 0)),
            pl.BlockSpec((G, LC), lambda i: (0, 0)),
        ],
        out_specs=[
            pl.BlockSpec((block_rows, KP), lambda i: (i, 0)),
            pl.BlockSpec((block_rows, KP), lambda i: (i, 0)),
            pl.BlockSpec((block_rows, LC), lambda i: (i, 0)),
        ],
        scratch_shapes=[pltpu.VMEM((KP, 2 * LC), bf16)],
        compiler_params=params(32),
        cost_estimate=pl.CostEstimate(
            flops=8 * NS * KP * LC, bytes_accessed=4 * NS * NS + 4 * NS * KP, transcendentals=0
        ),
        name="split",
    )(schur_block, left, pc, pg)

    outs = pl.pallas_call(
        first_kernel,
        out_shape=[seg_block] * 8
        + [shape(NS, LC), shape(CR, LC), shape(CR, LC), shape(CR, LC), shape(SLOTS, dtype=jnp.int32)]
        + [shape(8, LC), shape(G, LC), shape(G, LC)],
        in_specs=[VM] * 10 + [SM, ANY, ANY],
        out_specs=[VM] * 12 + [SM] + [VM] * 3,
        scratch_shapes=[
            pltpu.VMEM((CR, LC), f32),
            pltpu.VMEM((K_WIDE, 2 * LC), bf16),
            pltpu.VMEM((NS, K_WIDE), bf16),
            pltpu.VMEM((NS, K_WIDE), bf16),
            pltpu.SMEM((W * 8, 128), f32),
            pltpu.SemaphoreType.DMA((2, TILES)),
            pltpu.SemaphoreType.DMA((W,)),
        ],
        compiler_params=params(40),
        name="first",
    )(*incoming, blocks, left, pc, pg, partial, mask, source, high, low)
    forward, reply = outs[:4], outs[4:8]
    u0, term0, projected0, actives, slots, sums0, left_face, right_face = outs[8:]

    forward = [sent(forward[o], 1, o) for o in range(W)]
    back = [sent(reply[o], -1, -o) for o in range(W)]
    next_left = passed_along(left_face, -1)
    prev_right = passed_along(right_face, 1)
    sums0 = total(sums0)

    outs = pl.pallas_call(
        second_kernel,
        out_shape=[seg_block] * 4
        + [shape(NS, LC), shape(G, LC), shape(CR, LC), shape(8, LC), shape(G, LC)],
        in_specs=[SM] * 3 + [VM] * 20 + [ANY, ANY],
        out_specs=[VM] * 9,
        scratch_shapes=[
            pltpu.VMEM((CR, LC), f32),
            pltpu.VMEM((NS, LC), f32),
            pltpu.VMEM((KP, 2 * LC), bf16),
            pltpu.VMEM((NS, KP), bf16),
            pltpu.VMEM((NS, KP), bf16),
            pltpu.VMEM((CR, LC), f32),
            pltpu.SemaphoreType.DMA((2, TILES)),
        ],
        compiler_params=params(56),
        name="second",
    )(me, slots, place, *forward, *back, next_left, prev_right, u0, projected0, actives, mask,
      blocks, left, pc, pg, term0, sums0, high, low)
    reply, (u1, q_glue, q_contact, sums1, left_face) = outs[:4], outs[4:]

    back = [sent(reply[o], -1, -o) for o in range(W)]
    next_left = passed_along(left_face, -1)
    sums1 = total(sums1)

    mult_glue, mult_contact, res_glue, res_contact = pl.pallas_call(
        last_kernel,
        out_shape=[shape(G, LC), shape(CR, LC)] * 2,
        in_specs=[SM] + [VM] * 13,
        out_specs=[VM] * 4,
        compiler_params=params(24),
        name="last",
    )(place, *back, next_left, u1, q_glue, q_contact, pc, pg, mask, sums0, sums1)
    contact = (1, 1, SEG, SD, LC)
    return (
        mult_glue[None, None],
        mult_contact.reshape(contact),
        res_glue[None, None],
        res_contact.reshape(contact),
    )


def solution(mesh):
    in_specs = (
        P("body", "sub", None, None),
        P("body", "sub", None, None, None),
        P("body", "sub", None, None),
        P("body", "sub", None, None, None),
        P("body", "sub", None, None),
        P("body", "sub", None),
        P("body", "sub", None, None),
    )
    out_specs = (
        P("body", "sub", None, None),
        P("body", "sub", None, None, None),
        P("body", "sub", None, None),
        P("body", "sub", None, None, None),
    )
    return jax.shard_map(
        per_device, mesh=mesh, in_specs=in_specs, out_specs=out_specs, check_vma=False
    )
```

```python
import jax
import jax.numpy as jnp
from jax import lax
from jax.experimental import pallas as pl
from jax.experimental.pallas import tpu as pltpu
from jax.sharding import PartitionSpec as P

W = 4
CAP = 8
SLOTS = W * CAP
SEG = 16
SD = 64
LC = 128
G = 176
NS = 2400
CR = SEG * SD
MASTER = G + CR
RIGHT = G + 2 * CR
KP = 2560
K_LOW, K_WIDE = 1152, 1152
TILE = 480
TILES = NS // TILE
PIECE = 240
PIECES = NS // PIECE
DEPTH = 4
NEAR = CAP * SD
FAR = SEG * SD
MIB = 1 << 20

f32 = jnp.float32
bf16 = jnp.bfloat16
highest = lax.Precision.HIGHEST
VM = pl.BlockSpec(memory_space=pltpu.VMEM)
SM = pl.BlockSpec(memory_space=pltpu.SMEM)
ANY = pl.BlockSpec(memory_space=pl.ANY)


def rows(start, size):
    return pl.ds(pl.multiple_of(start, 8), size)


def halves(value):
    high = value.astype(bf16)
    low = (value - high.astype(f32)).astype(bf16)
    return high, low


def product(high, low, both):
    first = jnp.dot(high, both, preferred_element_type=f32)
    second = jnp.dot(low, both, preferred_element_type=f32)
    return (first[:, LC:] + second[:, LC:]) + second[:, :LC] + first[:, :LC]


def segment(index):
    return pl.ds(pl.multiple_of(index * SD, SD), SD)


def flag(condition):
    return jnp.where(condition, 1.0, 0.0).astype(f32)


def pack_kernel(
    me, owner, slot, act_any, rhs_any, glue_any,
    near, far, pc, mask, pg, near_source, far_source, place,
    act, rhs, act_wide, count, position, sems,
):
    copies = [
        pltpu.make_async_copy(src, dst, sems.at[i])
        for i, (src, dst) in enumerate(((act_any, act), (rhs_any, rhs), (glue_any, pg)))
    ]
    for copy in copies:
        copy.start()
    for i in range(SEG):
        far_source[i] = -1
    for n in range(CAP):
        near_source[n] = -1
    for o in range(W + 1):
        count[o] = 0
    for k in range(SEG):
        o = lax.rem(owner[k] - me[0] + 32, 32)
        n = count[o]
        q = count[W]
        count[o] = n + 1
        position[k] = o * CAP + n

        @pl.when(o == 0)
        def _():
            near_source[n] = k
            place[k] = n

        @pl.when(o > 0)
        def _():
            far_source[q] = k
            place[k] = CAP + q
            count[W] = q + 1

    for copy in copies:
        copy.wait()
    active = act[...].astype(f32)
    act_wide[...] = jnp.concatenate([active, jnp.zeros((SEG, 128 - SD), f32)], axis=1)
    columns = jnp.transpose(jnp.concatenate([act_wide[...], jnp.zeros((128 - SEG, 128), f32)], axis=0))
    for k in range(SEG):
        wide = jnp.broadcast_to(columns[:SD, k : k + 1], (SD, LC))
        here = slice(k * SD, (k + 1) * SD)
        mask[here, :] = wide
        pc[here, :] = rhs[here, :] * wide
    lane = lax.broadcasted_iota(jnp.int32, (1, 128), 1)
    for ref, source, slots in ((near, near_source, CAP), (far, far_source, SEG)):
        for n in range(slots):
            k = source[n]
            at = jnp.maximum(k, 0)
            used = flag(k >= 0)
            ref[n * SD : (n + 1) * SD, :] = pc[segment(at), :] * used
            tag = (slot[at] + 1).astype(f32)
            seat = position[at].astype(f32)
            row = jnp.where(lane == SD, tag, jnp.where(lane == SD + 1, seat, act_wide[pl.ds(at, 1), :]))
            ref[slots * SD + n : slots * SD + n + 1, :] = used * row


def spread(source, inverse, outs, info):
    for o in range(1, W):
        for n in range(CAP):
            q = inverse[o * CAP + n]
            at = jnp.maximum(q, 0)
            used = flag(q >= 0)
            outs[o - 1][n * SD : (n + 1) * SD, :] = source[segment(at), :] * used
            if info:
                outs[o - 1][NEAR + n : NEAR + n + 1, :] = source[pl.ds(FAR + at, 1), :] * used


def collect(route, replies, out):
    for q in range(SEG):
        o, n = lax.div(route[q], CAP), lax.rem(route[q], CAP)
        value = replies[1][segment(n), :]
        for w in (0, 2):
            value = jnp.where(o == w + 1, replies[w][segment(n), :], value)
        out[q * SD : (q + 1) * SD, :] = value


def fetch(place, near, far, k):
    seat = place[k]
    here = near[segment(jnp.minimum(seat, CAP - 1)), :]
    there = far[segment(jnp.maximum(seat - CAP, 0)), :]
    return jnp.where(seat < CAP, here, there)


def relay_kernel(far, token, out1, out2, out3, route, inverse, info, sem):
    copy = pltpu.make_async_copy(far.at[pl.ds(FAR, SEG), :], info, sem)
    copy.start()
    for i in range(SLOTS):
        inverse[i] = -1
    copy.wait()
    for q in range(SEG):
        seat = info[q, SD + 1].astype(jnp.int32)
        route[q] = seat

        @pl.when(seat > 0)
        def _():
            inverse[seat] = q

    spread(far, inverse, (out1, out2, out3), True)


def exchange_kernel(
    route, inverse, near_source, far, r1, r2, r3, u, mask, right, token0, token1,
    f1, f2, f3, back, near, face,
):
    spread(far, inverse, (f1, f2, f3), False)
    collect(route, (r1, r2, r3), back)
    for n in range(CAP):
        k = near_source[n]
        at = jnp.maximum(k, 0)
        near[n * SD : (n + 1) * SD, :] = u[rows(G + at * SD, SD), :] * mask[segment(at), :] * flag(k >= 0)
    face[...] = right[...]


def collect_kernel(route, r1, r2, r3, back):
    collect(route, (r1, r2, r3), back)


def split_kernel(
    c_any, left, pc, pg, mortar, high, low, partial, forth, back, both, tiles, sems
):
    def fetch(i):
        return pltpu.make_async_copy(
            c_any.at[pl.ds(i * PIECE, PIECE), :], tiles.at[i % DEPTH], sems.at[i % DEPTH]
        )

    for i in range(DEPTH - 1):
        fetch(i).start()
    both[...] = jnp.zeros_like(both)
    for start, size, ref, sign in ((0, G, left, -1.0), (G, CR, pc, 1.0), (RIGHT, G, pg, 1.0)):
        part_high, part_low = halves(ref[...] * sign)
        both[start : start + size, :LC] = part_high
        both[start : start + size, LC:] = part_low
    for j in range(SEG):
        block = mortar[j * SD : (j + 1) * SD, :]
        for ref, value in ((forth, -jnp.transpose(block)), (back, block)):
            part_high, part_low = halves(value)
            ref[2 * j * SD : (2 * j + 1) * SD, :] = part_high
            ref[(2 * j + 1) * SD : (2 * j + 2) * SD, :] = part_low
    for i in range(PIECES):
        if i + DEPTH - 1 < PIECES:
            fetch(i + DEPTH - 1).start()
        fetch(i).wait()
        at = slice(i * PIECE, (i + 1) * PIECE)
        part_high, part_low = halves(tiles[i % DEPTH])
        pad = jnp.zeros((PIECE, KP - NS), bf16)
        high[at, :NS] = part_high
        high[at, NS:] = pad
        low[at, :NS] = part_low
        low[at, NS:] = pad
        partial[at, :] = product(high[at, :], low[at, :], both[...])


def mortar_apply(mortar, j, value):
    part_high, part_low = halves(value)
    wide = jnp.concatenate([part_high, part_low], axis=1)
    parts = jnp.dot(mortar[2 * j * SD : (2 * j + 2) * SD, :], wide, preferred_element_type=f32)
    return (parts[SD:, LC:] + parts[SD:, :LC]) + parts[:SD, LC:] + parts[:SD, :LC]


def column_sum(value):
    return jnp.sum(value, axis=0, keepdims=True)


def first_kernel(
    in0, in1, in2, in3, forth, back, left, pc, pg, partial, mask, source, high, low,
    far, p0, p1, p2, p3, u, projected, actives, slots, sums, left_face, right_face,
    gathered, term, both, info, info_sems,
):
    ins = (in0, in1, in2, in3)
    infos = []
    for o in range(W):
        copy = pltpu.make_async_copy(ins[o].at[pl.ds(NEAR, 8), :], info.at[pl.ds(o * 8, 8), :], info_sems.at[o])
        copy.start()
        infos.append(copy)
    gathered[...] = jnp.zeros_like(gathered)
    actives[...] = jnp.zeros_like(actives)
    both[...] = jnp.zeros_like(both)
    for copy in infos:
        copy.wait()
    for o in range(W):
        tile = jnp.concatenate([ins[o][NEAR : NEAR + 8, :], jnp.zeros((120, 128), f32)], axis=0)
        columns = jnp.transpose(tile)
        for n in range(CAP):
            j = info[o * 8 + n, SD].astype(jnp.int32) - 1
            slots[o * CAP + n] = j
            at = rows(jnp.maximum(j, 0) * SD, SD)
            gathered[at, :] += ins[o][n * SD : (n + 1) * SD, :]
            actives[at, :] += jnp.broadcast_to(columns[:SD, n : n + 1], (SD, LC))
    for j in range(SEG):
        value = mortar_apply(forth, j, gathered[j * SD : (j + 1) * SD, :])
        term[j * SD : (j + 1) * SD, :] = value
        part_high, part_low = halves(value)
        start = MASTER - K_LOW + j * SD
        both[start : start + SD, :LC] = part_high
        both[start : start + SD, LC:] = part_low
    for i in range(TILES):
        at = slice(i * TILE, (i + 1) * TILE)
        u[at, :] = partial[at, :] + product(
            high[at, K_LOW : K_LOW + K_WIDE], low[at, K_LOW : K_LOW + K_WIDE], both[...]
        )
    left_face[...] = u[:G, :]
    right_face[...] = u[RIGHT:, :]
    for j in range(SEG):
        start = MASTER + j * SD
        projected[j * SD : (j + 1) * SD, :] = mortar_apply(back, j, u[start : start + SD, :])
    for q in range(SEG):
        k = source[q]
        at = jnp.maximum(k, 0)
        far[q * SD : (q + 1) * SD, :] = u[rows(G + at * SD, SD), :] * mask[segment(at), :] * flag(k >= 0)
    for o, reply in enumerate((p0, p1, p2, p3)):
        for n in range(CAP):
            j = jnp.maximum(slots[o * CAP + n], 0)
            reply[n * SD : (n + 1) * SD, :] = projected[segment(j), :]
    norm = column_sum(pg[...] * pg[...]) + column_sum(pc[...] * pc[...])
    curvature = (
        column_sum(pg[...] * u[RIGHT:, :])
        - column_sum(left[...] * u[:G, :])
        + column_sum(pc[...] * u[G:MASTER, :])
        + column_sum(term[...] * u[MASTER:RIGHT, :])
    )
    sums[...] = jnp.concatenate([norm, curvature, jnp.zeros((6, LC), f32)], axis=0)


def second_kernel(
    me, slots, place, f0, f1, f2, f3, near, far, next_left, prev_right, u0, projected0, actives, mask,
    forth, project, sums0, high, low,
    p0, p1, p2, p3, u, q_glue, q_contact, sums, left_face,
    gathered, loads, both, projected,
):
    forward, reply = (f0, f1, f2, f3), (p0, p1, p2, p3)
    inner = jnp.where(me[0] > 0, 1.0, 0.0).astype(f32)
    loads[:G, :] = (u0[:G, :] - prev_right[...]) * inner
    glue = u0[RIGHT:, :] - next_left[...]
    q_glue[...] = glue
    loads[RIGHT:, :] = glue
    gathered[...] = -(actives[...] * projected0[...])
    for o in range(W):
        for n in range(CAP):
            at = rows(jnp.maximum(slots[o * CAP + n], 0) * SD, SD)
            gathered[at, :] += forward[o][n * SD : (n + 1) * SD, :]
    for k in range(SEG):
        here = slice(k * SD, (k + 1) * SD)
        fetched = fetch(place, near, far, k)
        value = mask[here, :] * (u0[G + k * SD : G + (k + 1) * SD, :] - fetched)
        q_contact[here, :] = value
        loads[G + k * SD : G + (k + 1) * SD, :] = value
    for j in range(SEG):
        value = mortar_apply(forth, j, gathered[j * SD : (j + 1) * SD, :])
        loads[MASTER + j * SD : MASTER + (j + 1) * SD, :] = value
    part_high, part_low = halves(loads[...])
    both[:NS, :LC] = part_high
    both[:NS, LC:] = part_low
    both[NS:, :] = jnp.zeros((KP - NS, 2 * LC), bf16)
    for i in range(TILES):
        at = slice(i * TILE, (i + 1) * TILE)
        u[at, :] = product(high[at, :], low[at, :], both[...])
    left_face[...] = u[:G, :]
    for j in range(SEG):
        start = MASTER + j * SD
        projected[j * SD : (j + 1) * SD, :] = mortar_apply(project, j, u[start : start + SD, :])
    for o in range(W):
        for n in range(CAP):
            j = jnp.maximum(slots[o * CAP + n], 0)
            reply[o][n * SD : (n + 1) * SD, :] = projected[rows(j * SD, SD), :]
    square = column_sum(q_glue[...] * q_glue[...]) + column_sum(q_contact[...] * q_contact[...])
    energy = column_sum(loads[...] * u[...])
    sums[...] = jnp.concatenate([sums0[0:2, :], square, energy, jnp.zeros((4, LC), f32)], axis=0)


def last_kernel(
    place, near, far, next_left, u, q_glue, q_contact, pc, pg, mask, sums,
    mult_glue, mult_contact, res_glue, res_contact,
):
    norm0, curvature0, square, energy = (sums[i : i + 1, :] for i in range(4))
    alpha0 = norm0 / curvature0
    norm1 = (norm0 - alpha0 * curvature0) + alpha0 * (alpha0 * square - curvature0)
    own = (curvature0 - alpha0 * square) + alpha0 * (alpha0 * energy - square)
    cross = curvature0 - alpha0 * square
    ratio = norm1 / norm0
    curvature1 = own + ratio * (2.0 * cross + ratio * curvature0)
    alpha1 = norm1 / curvature1

    def finish(r0, q, w):
        r1 = r0 - alpha0 * q
        direction = r1 + ratio * r0
        image = (q - alpha0 * w) + ratio * q
        return alpha0 * r0 + alpha1 * direction, r1 - alpha1 * image

    mult, res = finish(pg[...], q_glue[...], u[RIGHT:, :] - next_left[...])
    mult_glue[...] = mult
    res_glue[...] = res
    for k in range(SEG):
        here = slice(k * SD, (k + 1) * SD)
        fetched = fetch(place, near, far, k)
        value = mask[here, :] * (u[G + k * SD : G + (k + 1) * SD, :] - fetched)
        mult, res = finish(pc[here, :], q_contact[here, :], value)
        mult_contact[here, :] = mult
        res_contact[here, :] = res


def shape(*dims, dtype=f32):
    return jax.ShapeDtypeStruct(dims, dtype)


def params(mib):
    return pltpu.CompilerParams(vmem_limit_bytes=mib * MIB)


def sent(value, body_step, sub_step):
    subs, bodies = lax.axis_size("sub"), lax.axis_size("body")
    pairs = [
        (s * bodies + b, ((s + sub_step) % subs) * bodies + (b + body_step) % bodies)
        for s in range(subs)
        for b in range(bodies)
    ]
    return lax.ppermute(value, ("sub", "body"), pairs)


def passed_along(value, steps):
    count = lax.axis_size("sub")
    first, last = (max(0, -steps), min(count, count - steps))
    return lax.ppermute(value, "sub", [(source, source + steps) for source in range(first, last)])


def rotated(value, block, stride, steps):
    count = lax.axis_size("sub")
    pairs = []
    for s in range(count):
        place = s // stride % block
        pairs.append((s, s + ((place + steps) % block - place) * stride))
    return lax.ppermute(value, "sub", pairs)


def total(value):
    value = value + sent(value, 1, 0) + sent(value, 2, 0) + sent(value, 3, 0)
    for stride in (8, 2):
        value = value + sum(rotated(value, 4, stride, k) for k in (1, 2, 3))
    return value + rotated(value, 2, 1, 1)


def kept(value):
    return pltpu.with_memory_space_constraint(value, pltpu.VMEM)


def per_device(compliance, mortar, rhs_glue, rhs_contact, owner_sub, master_slot, active_set):
    schur_block = compliance[0, 0]
    blocks = mortar.reshape(CR, SD)
    rhs = rhs_contact.reshape(CR, LC)
    me = lax.axis_index("sub").astype(jnp.int32).reshape(1)
    seg_block = shape(NEAR, LC)
    far_block = shape(FAR, LC)
    index = [shape(n, dtype=jnp.int32) for n in (CAP, SEG, SEG)]

    near, far, pc, mask, pg, near_source, far_source, place = pl.pallas_call(
        pack_kernel,
        out_shape=[shape(NEAR + CAP, LC), shape(FAR + SEG, LC)]
        + [shape(CR, LC)] * 2
        + [shape(G, LC)]
        + index,
        in_specs=[SM, SM, SM, ANY, ANY, ANY],
        out_specs=[VM] * 5 + [SM] * 3,
        scratch_shapes=[
            pltpu.VMEM((SEG, SD), jnp.int32),
            pltpu.VMEM((CR, LC), f32),
            pltpu.VMEM((SEG, 128), f32),
            pltpu.SMEM((W + 1,), jnp.int32),
            pltpu.SMEM((SEG,), jnp.int32),
            pltpu.SemaphoreType.DMA((3,)),
        ],
        compiler_params=params(8),
        name="pack",
    )(me, owner_sub.reshape(SEG), master_slot.reshape(SEG), active_set.reshape(SEG, SD), rhs, rhs_glue[0, 0])

    far_in = sent(far, 1, 2)
    near_in = sent(near, 1, 0)
    left = passed_along(pg, 1)

    stacked = shape(2 * CR, SD, dtype=bf16)
    high, low, partial, forth, project = pl.pallas_call(
        split_kernel,
        out_shape=[pltpu.VMEM((NS, KP), bf16)] * 2 + [shape(NS, LC), stacked, stacked],
        in_specs=[ANY] + [VM] * 4,
        out_specs=[VM] * 5,
        scratch_shapes=[
            pltpu.VMEM((KP, 2 * LC), bf16),
            pltpu.VMEM((DEPTH, PIECE, NS), f32),
            pltpu.SemaphoreType.DMA((DEPTH,)),
        ],
        compiler_params=params(20),
        cost_estimate=pl.CostEstimate(
            flops=8 * NS * KP * LC, bytes_accessed=4 * NS * NS, transcendentals=0
        ),
        name="split",
    )(schur_block, left, pc, pg, blocks)
    high, low = kept(high), kept(low)

    out1, kept2, out3, route, inverse = pl.pallas_call(
        relay_kernel,
        out_shape=[shape(NEAR + CAP, LC)] * 3 + [shape(SEG, dtype=jnp.int32), shape(SLOTS, dtype=jnp.int32)],
        in_specs=[VM, ANY],
        out_specs=[VM] * 3 + [SM] * 2,
        scratch_shapes=[pltpu.SMEM((SEG, 128), f32), pltpu.SemaphoreType.DMA],
        compiler_params=params(6),
        name="relay",
    )(far_in, partial)
    in1, in3 = sent(out1, 0, -1), sent(out3, 0, 1)

    outs = pl.pallas_call(
        first_kernel,
        out_shape=[far_block] + [seg_block] * 4
        + [shape(NS, LC), shape(CR, LC), shape(CR, LC), shape(SLOTS, dtype=jnp.int32)]
        + [shape(8, LC), shape(G, LC), shape(G, LC)],
        in_specs=[VM] * 11 + [SM, VM, VM],
        out_specs=[VM] * 8 + [SM] + [VM] * 3,
        scratch_shapes=[
            pltpu.VMEM((CR, LC), f32),
            pltpu.VMEM((CR, LC), f32),
            pltpu.VMEM((K_WIDE, 2 * LC), bf16),
            pltpu.SMEM((W * 8, 128), f32),
            pltpu.SemaphoreType.DMA((W,)),
        ],
        compiler_params=params(12),
        name="first",
    )(near_in, in1, kept2, in3, forth, project, left, pc, pg, partial, mask, far_source, high, low)
    far, replies = outs[0], outs[1:5]
    u0, projected0, actives, slots, sums0, left_face, right_face = outs[5:]

    far_in = sent(far, 1, 2)
    reply1, reply3 = sent(replies[1], 0, 1), sent(replies[3], 0, -1)
    near_back = sent(replies[0], -1, 0)
    next_left = passed_along(left_face, -1)

    out1, kept2, out3, far, near, right_face = pl.pallas_call(
        exchange_kernel,
        out_shape=[seg_block] * 3 + [far_block, seg_block, shape(G, LC)],
        in_specs=[SM] * 3 + [VM] * 7 + [ANY] * 2,
        out_specs=[VM] * 6,
        compiler_params=params(12),
        name="exchange",
    )(route, inverse, near_source, far_in, reply1, replies[2], reply3, u0, mask, right_face, near_back, next_left)
    far_back = sent(far, -1, -2)
    in1, in3 = sent(out1, 0, -1), sent(out3, 0, 1)
    near_in = sent(near, 1, 0)
    prev_right = passed_along(right_face, 1)

    outs = pl.pallas_call(
        second_kernel,
        out_shape=[seg_block] * 4
        + [shape(NS, LC), shape(G, LC), shape(CR, LC), shape(8, LC), shape(G, LC)],
        in_specs=[SM] * 3 + [VM] * 17,
        out_specs=[VM] * 9,
        scratch_shapes=[
            pltpu.VMEM((CR, LC), f32),
            pltpu.VMEM((NS, LC), f32),
            pltpu.VMEM((KP, 2 * LC), bf16),
            pltpu.VMEM((CR, LC), f32),
        ],
        compiler_params=params(12),
        name="second",
    )(me, slots, place, near_in, in1, kept2, in3, near_back, far_back, next_left, prev_right,
      u0, projected0, actives, mask, forth, project, sums0, high, low)
    replies, (u1, q_glue, q_contact, sums, left_face) = outs[:4], outs[4:]

    reply1, reply3 = sent(replies[1], 0, 1), sent(replies[3], 0, -1)
    near_back = sent(replies[0], -1, 0)
    next_left = passed_along(left_face, -1)
    sums = total(sums)

    far = pl.pallas_call(
        collect_kernel,
        out_shape=far_block,
        in_specs=[SM] + [VM] * 3,
        out_specs=VM,
        compiler_params=params(6),
        name="collect",
    )(route, reply1, replies[2], reply3)
    far_back = sent(far, -1, -2)

    mult_glue, mult_contact, res_glue, res_contact = pl.pallas_call(
        last_kernel,
        out_shape=[shape(G, LC), shape(CR, LC)] * 2,
        in_specs=[SM] + [VM] * 10,
        out_specs=[VM] * 4,
        compiler_params=params(24),
        name="last",
    )(place, near_back, far_back, next_left, u1, q_glue, q_contact, pc, pg, mask, sums)
    contact = (1, 1, SEG, SD, LC)
    return (
        mult_glue[None, None],
        mult_contact.reshape(contact),
        res_glue[None, None],
        res_contact.reshape(contact),
    )


def solution(mesh):
    in_specs = (
        P("body", "sub", None, None),
        P("body", "sub", None, None, None),
        P("body", "sub", None, None),
        P("body", "sub", None, None, None),
        P("body", "sub", None, None),
        P("body", "sub", None),
        P("body", "sub", None, None),
    )
    out_specs = (
        P("body", "sub", None, None),
        P("body", "sub", None, None, None),
        P("body", "sub", None, None),
        P("body", "sub", None, None, None),
    )
    return jax.shard_map(
        per_device, mesh=mesh, in_specs=in_specs, out_specs=out_specs, check_vma=False
    )
```

```python
import jax
import jax.numpy as jnp
from jax import lax
from jax.experimental import pallas as pl
from jax.experimental.pallas import tpu as pltpu
from jax.sharding import PartitionSpec as P

W = 4
CAP = 8
SLOTS = W * CAP
SEG = 16
SD = 64
LC = 128
G = 176
NS = 2400
CR = SEG * SD
MASTER = G + CR
RIGHT = G + 2 * CR
KP = 2560
K_LOW, K_WIDE = 1152, 1152
K_LEFT = 256
K_NEAR = 1280
K_RIGHT = 2176
K_PAD = 256
HOP = 1
BACK_HOP = 1
TILE = 480
TILES = NS // TILE
PIECE = 240
PIECES = NS // PIECE
DEPTH = 4
NEAR = CAP * SD
FAR = SEG * SD
NSUB = 32
MIB = 1 << 20

f32 = jnp.float32
bf16 = jnp.bfloat16
highest = lax.Precision.HIGHEST
VM = pl.BlockSpec(memory_space=pltpu.VMEM)
SM = pl.BlockSpec(memory_space=pltpu.SMEM)
ANY = pl.BlockSpec(memory_space=pl.ANY)


def rows(start, size):
    return pl.ds(pl.multiple_of(start, 8), size)


def halves(value):
    high = value.astype(bf16)
    low = (value - high.astype(f32)).astype(bf16)
    return high, low


def product(high, low, both):
    first = jnp.dot(high, both, preferred_element_type=f32)
    second = jnp.dot(low, both, preferred_element_type=f32)
    return (first[:, LC:] + second[:, LC:]) + second[:, :LC] + first[:, :LC]


def segment(index):
    return pl.ds(pl.multiple_of(index * SD, SD), SD)


def flag(condition):
    return jnp.where(condition, 1.0, 0.0).astype(f32)


def put_slots(ref, source, slots, pc, act_wide, slot, position):
    lane = lax.broadcasted_iota(jnp.int32, (1, 128), 1)
    for n in range(slots):
        k = source[n]
        at = jnp.maximum(k, 0)
        used = flag(k >= 0)
        ref[n * SD : (n + 1) * SD, :] = pc[segment(at), :] * used
        tag = (slot[at] + 1).astype(f32)
        seat = position[at].astype(f32)
        row = jnp.where(lane == SD, tag, jnp.where(lane == SD + 1, seat, act_wide[pl.ds(at, 1), :]))
        ref[slots * SD + n : slots * SD + n + 1, :] = used * row


def pack_kernel(
    me, owner_any, slot_any, act_any, rhs_any, glue_any,
    far, pc, mask, pg, act_wide, near_source, far_source, place, position, slot,
    owner, act, rhs, count, sems,
):
    pairs = ((owner_any, owner), (slot_any, slot), (act_any, act), (rhs_any, rhs), (glue_any, pg))
    copies = [pltpu.make_async_copy(src, dst, sems.at[i]) for i, (src, dst) in enumerate(pairs)]
    for copy in copies:
        copy.start()
    for i in range(SEG):
        far_source[i] = -1
    for n in range(CAP):
        near_source[n] = -1
    for o in range(W + 1):
        count[o] = 0
    copies[0].wait()
    for k in range(SEG):
        o = lax.rem(owner[k] - me[0] + NSUB, NSUB)
        n = count[o]
        q = count[W]
        count[o] = n + 1
        position[k] = o * CAP + n

        @pl.when(o == 0)
        def _():
            near_source[n] = k
            place[k] = n

        @pl.when(o > 0)
        def _():
            far_source[q] = k
            place[k] = CAP + q
            count[W] = q + 1

    for copy in copies[1:]:
        copy.wait()
    active = act[...].astype(f32)
    act_wide[...] = jnp.concatenate([active, jnp.zeros((SEG, 128 - SD), f32)], axis=1)
    columns = jnp.transpose(jnp.concatenate([act_wide[...], jnp.zeros((128 - SEG, 128), f32)], axis=0))
    for k in range(SEG):
        wide = jnp.broadcast_to(columns[:SD, k : k + 1], (SD, LC))
        here = slice(k * SD, (k + 1) * SD)
        mask[here, :] = wide
        pc[here, :] = rhs[here, :] * wide
    put_slots(far, far_source, SEG, pc, act_wide, slot, position)


def read_route(info, first, route, inverse):
    for i in range(SLOTS):
        inverse[i] = -1
    for q in range(SEG):
        seat = info[first + q, SD + 1].astype(jnp.int32)
        if route is not None:
            route[q] = seat

        @pl.when(seat > 0)
        def _():
            inverse[seat] = q


def spread(source, inverse, outs, info):
    for o in range(1, W):
        for n in range(CAP):
            q = inverse[o * CAP + n]
            at = jnp.maximum(q, 0)
            used = flag(q >= 0)
            outs[o - 1][n * SD : (n + 1) * SD, :] = source[segment(at), :] * used
            if info:
                outs[o - 1][NEAR + n : NEAR + n + 1, :] = source[pl.ds(FAR + at, 1), :] * used


def collect(route, replies, out):
    for q in range(SEG):
        o, n = lax.div(route[q], CAP), lax.rem(route[q], CAP)
        value = replies[1][segment(n), :]
        for w in (0, 2):
            value = jnp.where(o == w + 1, replies[w][segment(n), :], value)
        out[q * SD : (q + 1) * SD, :] = value


def fetch(place, near, far, k):
    seat = place[k]
    here = near[segment(jnp.minimum(seat, CAP - 1)), :]
    there = far[segment(jnp.maximum(seat - CAP, 0)), :]
    return jnp.where(seat < CAP, here, there)


def relay_kernel(far, pg, token, out1, out2, out3, inverse, info, sem):
    copy = pltpu.make_async_copy(far.at[pl.ds(FAR, SEG), :], info, sem)
    copy.start()
    copy.wait()
    outs = (out1, out2, out3)
    read_route(info, 0, None, inverse)
    spread(far, inverse, outs, True)
    out1[NEAR + CAP : NEAR + CAP + SEG, :] = far[FAR:, :]
    outs[HOP][NEAR + CAP :, :] = pg[...]


def exchange_kernel(
    route, inverse, near_source, far, r1, r2, r3, u, mask, token,
    f1, f2, f3, back, near,
):
    spread(far, inverse, (f1, f2, f3), False)
    f2[NEAR:, :] = u[RIGHT:, :]
    collect(route, (r1, r2, r3), back)
    for n in range(CAP):
        k = near_source[n]
        at = jnp.maximum(k, 0)
        near[n * SD : (n + 1) * SD, :] = u[rows(G + at * SD, SD), :] * mask[segment(at), :] * flag(k >= 0)


def select_kernel(near, u, token, s0, s1, s2, s3, info, sem):
    copy = pltpu.make_async_copy(near.at[pl.ds(CR, 8), :], info, sem)
    copy.start()
    copy.wait()
    for o, out in enumerate((s0, s1, s2, s3)):
        for n in range(CAP):
            j = info[0, o * CAP + n].astype(jnp.int32)
            out[n * SD : (n + 1) * SD, :] = near[segment(j), :]
    s2[NEAR:, :] = u[:G, :]


def split_kernel(
    near_source, position, slot, c_any, pc, pg, mortar, act_wide,
    high, low, partial, forth, back, near, both, tiles, sems,
):
    def fetch(i):
        return pltpu.make_async_copy(
            c_any.at[pl.ds(i * PIECE, PIECE), :], tiles.at[i % DEPTH], sems.at[i % DEPTH]
        )

    for i in range(DEPTH - 1):
        fetch(i).start()
    put_slots(near, near_source, CAP, pc, act_wide, slot, position)
    both[...] = jnp.zeros_like(both)
    for start, size, ref in ((G, CR, pc), (RIGHT, G, pg)):
        part_high, part_low = halves(ref[...])
        both[start : start + size, :LC] = part_high
        both[start : start + size, LC:] = part_low
    for j in range(SEG):
        block = mortar[j * SD : (j + 1) * SD, :]
        for ref, value in ((forth, -jnp.transpose(block)), (back, block)):
            part_high, part_low = halves(value)
            ref[2 * j * SD : (2 * j + 1) * SD, :] = part_high
            ref[(2 * j + 1) * SD : (2 * j + 2) * SD, :] = part_low
    for i in range(PIECES):
        if i + DEPTH - 1 < PIECES:
            fetch(i + DEPTH - 1).start()
        fetch(i).wait()
        at = slice(i * PIECE, (i + 1) * PIECE)
        part_high, part_low = halves(tiles[i % DEPTH])
        pad = jnp.zeros((PIECE, KP - NS), bf16)
        high[at, :NS] = part_high
        high[at, NS:] = pad
        low[at, :NS] = part_low
        low[at, NS:] = pad
        partial[at, :] = product(high[at, :], low[at, :], both[...])


def mortar_apply(mortar, j, value):
    part_high, part_low = halves(value)
    wide = jnp.concatenate([part_high, part_low], axis=1)
    parts = jnp.dot(mortar[2 * j * SD : (2 * j + 2) * SD, :], wide, preferred_element_type=f32)
    return (parts[SD:, LC:] + parts[SD:, :LC]) + parts[:SD, LC:] + parts[:SD, :LC]


def column_sum(value):
    return jnp.sum(value, axis=0, keepdims=True)


def first_kernel(
    me, in0, in1, in2, in3, forth, back, pc, pg, partial, mask, source, high, low,
    far, p0, p1, p2, p3, u, projected, actives, slots, route, inverse, sums,
    gathered, term, both, info, info_sems,
):
    ins = (in0, in1, in2, in3)
    infos = []
    for o in range(W):
        copy = pltpu.make_async_copy(ins[o].at[pl.ds(NEAR, 8), :], info.at[pl.ds(o * 8, 8), :], info_sems.at[o])
        copy.start()
        infos.append(copy)
    gathered[...] = jnp.zeros_like(gathered)
    actives[...] = jnp.zeros_like(actives)
    both[...] = jnp.zeros_like(both)
    left = -ins[HOP + 1][NEAR + CAP :, :] * flag(me[0] > 0)
    part_high, part_low = halves(left)
    both[:G, :LC] = part_high
    both[:G, LC:] = part_low
    copy = pltpu.make_async_copy(
        in1.at[pl.ds(NEAR + CAP, SEG), :], info.at[pl.ds(W * 8, SEG), :], info_sems.at[W]
    )
    copy.start()
    infos.append(copy)
    for copy in infos:
        copy.wait()
    read_route(info, W * 8, route, inverse)
    for o in range(W):
        tile = jnp.concatenate([ins[o][NEAR : NEAR + 8, :], jnp.zeros((120, 128), f32)], axis=0)
        columns = jnp.transpose(tile)
        for n in range(CAP):
            j = info[o * 8 + n, SD].astype(jnp.int32) - 1
            slots[o * CAP + n] = j
            at = rows(jnp.maximum(j, 0) * SD, SD)
            gathered[at, :] += ins[o][n * SD : (n + 1) * SD, :]
            actives[at, :] += jnp.broadcast_to(columns[:SD, n : n + 1], (SD, LC))
    for j in range(SEG):
        value = mortar_apply(forth, j, gathered[j * SD : (j + 1) * SD, :])
        term[j * SD : (j + 1) * SD, :] = value
        part_high, part_low = halves(value)
        start = K_LEFT + MASTER - K_LOW + j * SD
        both[start : start + SD, :LC] = part_high
        both[start : start + SD, LC:] = part_low
    for i in range(TILES):
        at = slice(i * TILE, (i + 1) * TILE)
        wide = slice(K_LOW, K_LOW + K_WIDE)
        u[at, :] = (
            partial[at, :]
            + product(high[at, :K_LEFT], low[at, :K_LEFT], both[:K_LEFT, :])
            + product(high[at, wide], low[at, wide], both[K_LEFT:, :])
        )
    p2[NEAR:, :] = u[:G, :]
    for j in range(SEG):
        start = MASTER + j * SD
        projected[j * SD : (j + 1) * SD, :] = mortar_apply(back, j, u[start : start + SD, :])
    for q in range(SEG):
        k = source[q]
        at = jnp.maximum(k, 0)
        far[q * SD : (q + 1) * SD, :] = u[rows(G + at * SD, SD), :] * mask[segment(at), :] * flag(k >= 0)
    for o, reply in enumerate((p0, p1, p2, p3)):
        for n in range(CAP):
            j = jnp.maximum(slots[o * CAP + n], 0)
            reply[n * SD : (n + 1) * SD, :] = projected[segment(j), :]
    norm = column_sum(pg[...] * pg[...]) + column_sum(pc[...] * pc[...])
    curvature = (
        column_sum(pg[...] * u[RIGHT:, :])
        + column_sum(left * u[:G, :])
        + column_sum(pc[...] * u[G:MASTER, :])
        + column_sum(term[...] * u[MASTER:RIGHT, :])
    )
    sums[...] = jnp.concatenate([norm, curvature, jnp.zeros((6, LC), f32)], axis=0)


def master_kernel(
    slots, f0, f1, f2, f3, projected0, actives, forth, high, low, partial, term, gathered, both
):
    gathered[...] = -(actives[...] * projected0[...])
    for o, source in enumerate((f0, f1, f2, f3)):
        for n in range(CAP):
            at = segment(jnp.maximum(slots[o * CAP + n], 0))
            gathered[at, :] += source[n * SD : (n + 1) * SD, :]
    both[...] = jnp.zeros_like(both)
    for j in range(SEG):
        value = mortar_apply(forth, j, gathered[j * SD : (j + 1) * SD, :])
        term[j * SD : (j + 1) * SD, :] = value
        part_high, part_low = halves(value)
        start = MASTER - K_LOW + j * SD
        both[start : start + SD, :LC] = part_high
        both[start : start + SD, LC:] = part_low
    wide = slice(K_LOW, K_LOW + K_WIDE)
    for i in range(TILES):
        at = slice(i * TILE, (i + 1) * TILE)
        partial[at, :] = product(high[at, wide], low[at, wide], both[...])


def second_kernel(
    me, place, near, far, r2, f2, u0, mask, partial, term, sums0, high, low,
    u, q_glue, q_contact, sums,
    loads, both,
):
    loads[:G, :] = (u0[:G, :] - f2[NEAR:, :]) * flag(me[0] > 0)
    glue = u0[RIGHT:, :] - r2[NEAR:, :] * flag(me[0] < NSUB - 1)
    q_glue[...] = glue
    for k in range(SEG):
        here = slice(k * SD, (k + 1) * SD)
        fetched = fetch(place, near, far, k)
        value = mask[here, :] * (u0[G + k * SD : G + (k + 1) * SD, :] - fetched)
        q_contact[here, :] = value
        loads[G + k * SD : G + (k + 1) * SD, :] = value
    loads[MASTER:K_NEAR, :] = jnp.zeros((K_NEAR - MASTER, LC), f32)
    both[K_NEAR:, :] = jnp.zeros((K_PAD, 2 * LC), bf16)
    start = K_NEAR + RIGHT - K_RIGHT
    for at, value in ((slice(0, K_NEAR), loads[...]), (slice(start, start + G), glue)):
        part_high, part_low = halves(value)
        both[at, :LC] = part_high
        both[at, LC:] = part_low
    tail = slice(K_RIGHT, K_RIGHT + K_PAD)
    for i in range(TILES):
        at = slice(i * TILE, (i + 1) * TILE)
        u[at, :] = (
            partial[at, :]
            + product(high[at, :K_NEAR], low[at, :K_NEAR], both[:K_NEAR, :])
            + product(high[at, tail], low[at, tail], both[K_NEAR:, :])
        )
    square = column_sum(glue * glue) + column_sum(q_contact[...] * q_contact[...])
    energy = (
        column_sum(loads[:MASTER, :] * u[:MASTER, :])
        + column_sum(term[...] * u[MASTER:RIGHT, :])
        + column_sum(glue * u[RIGHT:, :])
    )
    sums[...] = jnp.concatenate([sums0[0:2, :], square, energy, jnp.zeros((4, LC), f32)], axis=0)


def reply_kernel(slots, project, u, sums, out, kept):
    kept[...] = sums[...]
    for j in range(SEG):
        start = MASTER + j * SD
        out[j * SD : (j + 1) * SD, :] = mortar_apply(project, j, u[start : start + SD, :])
    lane = lax.broadcasted_iota(jnp.int32, (8, 128), 1)
    row = jnp.zeros((8, 128), f32)
    for i in range(SLOTS):
        row = jnp.where(lane == i, jnp.maximum(slots[i], 0).astype(f32), row)
    out[CR:, :] = row


def last_kernel(
    me, position, s0, s1, s2, s3, u, q_glue, q_contact, pc, pg, mask, sums,
    mult_glue, mult_contact, res_glue, res_contact,
):
    norm0, curvature0, square, energy = (sums[i : i + 1, :] for i in range(4))
    alpha0 = norm0 / curvature0
    norm1 = (norm0 - alpha0 * curvature0) + alpha0 * (alpha0 * square - curvature0)
    own = (curvature0 - alpha0 * square) + alpha0 * (alpha0 * energy - square)
    cross = curvature0 - alpha0 * square
    ratio = norm1 / norm0
    curvature1 = own + ratio * (2.0 * cross + ratio * curvature0)
    alpha1 = norm1 / curvature1

    def finish(r0, q, w):
        r1 = r0 - alpha0 * q
        direction = r1 + ratio * r0
        image = (q - alpha0 * w) + ratio * q
        return alpha0 * r0 + alpha1 * direction, r1 - alpha1 * image

    mult, res = finish(pg[...], q_glue[...], u[RIGHT:, :] - s2[NEAR:, :] * flag(me[0] < NSUB - 1))
    mult_glue[...] = mult
    res_glue[...] = res
    for k in range(SEG):
        here = slice(k * SD, (k + 1) * SD)
        o, n = lax.div(position[k], CAP), lax.rem(position[k], CAP)
        fetched = s0[segment(n), :]
        for w, ref in ((1, s1), (2, s2), (3, s3)):
            fetched = jnp.where(o == w, ref[segment(n), :], fetched)
        value = mask[here, :] * (u[G + k * SD : G + (k + 1) * SD, :] - fetched)
        mult, res = finish(pc[here, :], q_contact[here, :], value)
        mult_contact[here, :] = mult
        res_contact[here, :] = res


def shape(*dims, dtype=f32):
    return jax.ShapeDtypeStruct(dims, dtype)


def params(mib):
    return pltpu.CompilerParams(vmem_limit_bytes=mib * MIB)


def sent(value, body_step, sub_step):
    subs, bodies = lax.axis_size("sub"), lax.axis_size("body")
    pairs = [
        (s * bodies + b, ((s + sub_step) % subs) * bodies + (b + body_step) % bodies)
        for s in range(subs)
        for b in range(bodies)
    ]
    return lax.ppermute(value, ("sub", "body"), pairs)


def moved(value, body_step, sub_step):
    return sent(value, body_step, sub_step) if body_step or sub_step else value


def rotated(value, block, stride, steps):
    count = lax.axis_size("sub")
    pairs = []
    for s in range(count):
        place = s // stride % block
        pairs.append((s, s + ((place + steps) % block - place) * stride))
    return lax.ppermute(value, "sub", pairs)


def total(value):
    value = value + sum(rotated(value, 4, 2, k) for k in (1, 2, 3))
    value = value + rotated(value, 2, 1, 1)
    value = value + sum(rotated(value, 4, 8, k) for k in (1, 2, 3))
    token = value
    value = value + sent(value, 1, 0) + sent(value, 2, 0) + sent(value, 3, 0)
    return value, token


def in_hbm(value):
    return pltpu.with_memory_space_constraint(value, pltpu.HBM)


def kept(value):
    return pltpu.with_memory_space_constraint(value, pltpu.VMEM)


def per_device(compliance, mortar, rhs_glue, rhs_contact, owner_sub, master_slot, active_set):
    schur_block = compliance[0, 0]
    blocks = mortar.reshape(CR, SD)
    rhs = rhs_contact.reshape(CR, LC)
    me = lax.axis_index("sub").astype(jnp.int32).reshape(1)
    seg_block = shape(NEAR, LC)
    far_block = shape(FAR, LC)
    info_block = shape(NEAR + CAP, LC)
    face_block = shape(NEAR + G, LC)

    def index(n):
        return shape(n, dtype=jnp.int32)

    far, pc, mask, pg, act_wide, near_source, far_source, place, position, slot = pl.pallas_call(
        pack_kernel,
        out_shape=[shape(FAR + SEG, LC), shape(CR, LC), shape(CR, LC), shape(G, LC), shape(SEG, 128)]
        + [index(n) for n in (CAP, SEG, SEG, SEG, SEG)],
        in_specs=[SM] + [ANY] * 5,
        out_specs=[VM] * 5 + [SM] * 5,
        scratch_shapes=[
            pltpu.SMEM((SEG,), jnp.int32),
            pltpu.VMEM((SEG, SD), jnp.int32),
            pltpu.VMEM((CR, LC), f32),
            pltpu.SMEM((W + 1,), jnp.int32),
            pltpu.SemaphoreType.DMA((5,)),
        ],
        compiler_params=params(8),
        name="pack",
    )(me, *(in_hbm(v) for v in (
        owner_sub.reshape(SEG), master_slot.reshape(SEG), active_set.reshape(SEG, SD), rhs, rhs_glue[0, 0],
    )))

    far_in = sent(far, 1, HOP)

    stacked = shape(2 * CR, SD, dtype=bf16)
    high, low, partial, forth, project, near = pl.pallas_call(
        split_kernel,
        out_shape=[pltpu.VMEM((NS, KP), bf16)] * 2 + [shape(NS, LC), stacked, stacked, info_block],
        in_specs=[SM] * 3 + [ANY] + [VM] * 4,
        out_specs=[VM] * 6,
        scratch_shapes=[
            pltpu.VMEM((KP, 2 * LC), bf16),
            pltpu.VMEM((DEPTH, PIECE, NS), f32),
            pltpu.SemaphoreType.DMA((DEPTH,)),
        ],
        compiler_params=params(20),
        cost_estimate=pl.CostEstimate(
            flops=8 * NS * KP * LC, bytes_accessed=4 * NS * NS, transcendentals=0
        ),
        name="split",
    )(near_source, position, slot, in_hbm(schur_block), pc, pg, blocks, act_wide)
    high, low = kept(high), kept(low)
    near_in = sent(near, 1, 0)

    relayed = [shape(NEAR + CAP + extra, LC) for extra in ((SEG, 0, G) if HOP == 2 else (SEG, G, 0))]
    outgoing = pl.pallas_call(
        relay_kernel,
        out_shape=relayed + [index(SLOTS)],
        in_specs=[VM, VM, ANY],
        out_specs=[VM] * 3 + [SM],
        scratch_shapes=[pltpu.SMEM((SEG, 128), f32), pltpu.SemaphoreType.DMA],
        compiler_params=params(6),
        name="relay",
    )(far_in, pg, partial)
    incoming = [near_in] + [moved(outgoing[o - 1], 0, o - HOP) for o in range(1, W)]

    outs = pl.pallas_call(
        first_kernel,
        out_shape=[far_block, seg_block, seg_block, face_block, seg_block]
        + [shape(NS, LC), shape(CR, LC), shape(CR, LC)]
        + [index(SLOTS), index(SEG), index(SLOTS), shape(8, LC)],
        in_specs=[SM] + [VM] * 10 + [SM, VM, VM],
        out_specs=[VM] * 8 + [SM] * 3 + [VM],
        scratch_shapes=[
            pltpu.VMEM((CR, LC), f32),
            pltpu.VMEM((CR, LC), f32),
            pltpu.VMEM((K_LEFT + K_WIDE, 2 * LC), bf16),
            pltpu.SMEM((W * 8 + SEG, 128), f32),
            pltpu.SemaphoreType.DMA((W + 1,)),
        ],
        compiler_params=params(12),
        name="first",
    )(me, *incoming, forth, project, pc, pg, partial, mask, far_source, high, low)
    far, replies = outs[0], outs[1:5]
    u0, projected0, actives, slots, route, inverse, sums0 = outs[5:]

    far_in = sent(far, 1, BACK_HOP)
    replies = [sent(replies[0], -1, 0)] + [moved(replies[o], 0, BACK_HOP - o) for o in range(1, W)]
    near_back, next_left = replies[0], replies[2]

    *outgoing, far, near = pl.pallas_call(
        exchange_kernel,
        out_shape=[seg_block, face_block, seg_block, far_block, seg_block],
        in_specs=[SM] * 3 + [VM] * 6 + [ANY],
        out_specs=[VM] * 5,
        compiler_params=params(12),
        name="exchange",
    )(route, inverse, near_source, far_in, *replies[1:], u0, mask, near_back)
    far_back = sent(far, -1, -BACK_HOP)
    incoming = [sent(near, 1, 0)] + [moved(outgoing[o - 1], 0, o - BACK_HOP) for o in range(1, W)]

    partial, term = pl.pallas_call(
        master_kernel,
        out_shape=[shape(NS, LC), shape(CR, LC)],
        in_specs=[SM] + [VM] * 9,
        out_specs=[VM] * 2,
        scratch_shapes=[pltpu.VMEM((CR, LC), f32), pltpu.VMEM((K_WIDE, 2 * LC), bf16)],
        compiler_params=params(12),
        cost_estimate=pl.CostEstimate(flops=8 * NS * K_WIDE * LC, bytes_accessed=MIB, transcendentals=0),
        name="master",
    )(slots, *incoming, projected0, actives, forth, high, low)

    u1, q_glue, q_contact, sums = pl.pallas_call(
        second_kernel,
        out_shape=[shape(NS, LC), shape(G, LC), shape(CR, LC), shape(8, LC)],
        in_specs=[SM] * 2 + [VM] * 11,
        out_specs=[VM] * 4,
        scratch_shapes=[pltpu.VMEM((K_NEAR, LC), f32), pltpu.VMEM((K_NEAR + K_PAD, 2 * LC), bf16)],
        compiler_params=params(12),
        name="second",
    )(me, place, near_back, far_back, next_left, incoming[2], u0, mask, partial, term, sums0, high, low)

    replied, sums = pl.pallas_call(
        reply_kernel,
        out_shape=[shape(CR + 8, LC), shape(8, LC)],
        in_specs=[SM] + [VM] * 3,
        out_specs=[VM] * 2,
        compiler_params=params(8),
        cost_estimate=pl.CostEstimate(flops=0, bytes_accessed=8 * MIB, transcendentals=0),
        name="reply",
    )(slots, project, u1, sums)
    replied = sent(replied, -1, -1)
    sums, token = total(sums)

    *outgoing, = pl.pallas_call(
        select_kernel,
        out_shape=[seg_block, seg_block, face_block, seg_block],
        in_specs=[VM] * 2 + [ANY],
        out_specs=[VM] * 4,
        scratch_shapes=[pltpu.SMEM((8, 128), f32), pltpu.SemaphoreType.DMA],
        compiler_params=params(6),
        name="select",
    )(replied, u1, token)
    fetched = [moved(outgoing[o], 0, 1 - o) for o in range(W)]

    mult_glue, mult_contact, res_glue, res_contact = pl.pallas_call(
        last_kernel,
        out_shape=[shape(G, LC), shape(CR, LC)] * 2,
        in_specs=[SM] * 2 + [VM] * 11,
        out_specs=[VM] * 4,
        compiler_params=params(24),
        name="last",
    )(me, position, *fetched, u1, q_glue, q_contact, pc, pg, mask, sums)
    contact = (1, 1, SEG, SD, LC)
    return (
        mult_glue[None, None],
        mult_contact.reshape(contact),
        res_glue[None, None],
        res_contact.reshape(contact),
    )


def solution(mesh):
    in_specs = (
        P("body", "sub", None, None),
        P("body", "sub", None, None, None),
        P("body", "sub", None, None),
        P("body", "sub", None, None, None),
        P("body", "sub", None, None),
        P("body", "sub", None),
        P("body", "sub", None, None),
    )
    out_specs = (
        P("body", "sub", None, None),
        P("body", "sub", None, None, None),
        P("body", "sub", None, None),
        P("body", "sub", None, None, None),
    )
    return jax.shard_map(
        per_device, mesh=mesh, in_specs=in_specs, out_specs=out_specs, check_vma=False
    )
```

```python
import jax
import jax.numpy as jnp
from jax import lax
from jax.experimental import pallas as pl
from jax.experimental.pallas import tpu as pltpu
from jax.sharding import PartitionSpec as P

W = 4
CAP = 8
SLOTS = W * CAP
SEG = 16
SD = 64
LC = 128
G = 176
NS = 2400
CR = SEG * SD
MASTER = G + CR
RIGHT = G + 2 * CR
KP = 2560
K_LOW, K_WIDE = 1152, 1152
K_LEFT = 256
K_NEAR = 1280
K_RIGHT = 2176
K_PAD = 256
HOP = 1
BACK_HOP = 1
TILE = 240
TILES = NS // TILE
PIECE = 240
PIECES = NS // PIECE
DEPTH = 4
NEAR = CAP * SD
FAR = SEG * SD
NSUB = 32
MIB = 1 << 20

f32 = jnp.float32
bf16 = jnp.bfloat16
highest = lax.Precision.HIGHEST
VM = pl.BlockSpec(memory_space=pltpu.VMEM)
SM = pl.BlockSpec(memory_space=pltpu.SMEM)
ANY = pl.BlockSpec(memory_space=pl.ANY)


def rows(start, size):
    return pl.ds(pl.multiple_of(start, 8), size)


def halves(value):
    high = value.astype(bf16)
    low = (value - high.astype(f32)).astype(bf16)
    return high, low


def product(high, low, both):
    first = jnp.dot(high, both, preferred_element_type=f32)
    second = jnp.dot(low, both, preferred_element_type=f32)
    return (first[:, LC:] + second[:, LC:]) + second[:, :LC] + first[:, :LC]


def segment(index):
    return pl.ds(pl.multiple_of(index * SD, SD), SD)


def flag(condition):
    return jnp.where(condition, 1.0, 0.0).astype(f32)


def put_slots(ref, source, slots, pc, act_wide, slot, position):
    lane = lax.broadcasted_iota(jnp.int32, (1, 128), 1)
    for n in range(slots):
        k = source[n]
        at = jnp.maximum(k, 0)
        used = flag(k >= 0)
        ref[n * SD : (n + 1) * SD, :] = pc[segment(at), :] * used
        tag = (slot[at] + 1).astype(f32)
        seat = position[at].astype(f32)
        row = jnp.where(lane == SD, tag, jnp.where(lane == SD + 1, seat, act_wide[pl.ds(at, 1), :]))
        ref[slots * SD + n : slots * SD + n + 1, :] = used * row


def pack_kernel(
    me, owner_any, slot_any, act_any, rhs_any, glue_any,
    far, pc, mask, pg, act_wide, near_source, far_source, place, position, slot,
    owner, act, rhs, count, sems,
):
    pairs = ((owner_any, owner), (slot_any, slot), (act_any, act), (rhs_any, rhs), (glue_any, pg))
    copies = [pltpu.make_async_copy(src, dst, sems.at[i]) for i, (src, dst) in enumerate(pairs)]
    for copy in copies:
        copy.start()
    for i in range(SEG):
        far_source[i] = -1
    for n in range(CAP):
        near_source[n] = -1
    for o in range(W + 1):
        count[o] = 0
    copies[0].wait()
    for k in range(SEG):
        o = lax.rem(owner[k] - me[0] + NSUB, NSUB)
        n = count[o]
        q = count[W]
        count[o] = n + 1
        position[k] = o * CAP + n

        @pl.when(o == 0)
        def _():
            near_source[n] = k
            place[k] = n

        @pl.when(o > 0)
        def _():
            far_source[q] = k
            place[k] = CAP + q
            count[W] = q + 1

    for copy in copies[1:]:
        copy.wait()
    active = act[...].astype(f32)
    act_wide[...] = jnp.concatenate([active, jnp.zeros((SEG, 128 - SD), f32)], axis=1)
    columns = jnp.transpose(jnp.concatenate([act_wide[...], jnp.zeros((128 - SEG, 128), f32)], axis=0))
    for k in range(SEG):
        wide = jnp.broadcast_to(columns[:SD, k : k + 1], (SD, LC))
        here = slice(k * SD, (k + 1) * SD)
        mask[here, :] = wide
        pc[here, :] = rhs[here, :] * wide
    put_slots(far, far_source, SEG, pc, act_wide, slot, position)


def read_route(info, first, route, inverse):
    for i in range(SLOTS):
        inverse[i] = -1
    for q in range(SEG):
        seat = info[first + q, SD + 1].astype(jnp.int32)
        if route is not None:
            route[q] = seat

        @pl.when(seat > 0)
        def _():
            inverse[seat] = q


def spread(source, inverse, outs, info):
    for o in range(1, W):
        for n in range(CAP):
            q = inverse[o * CAP + n]
            at = jnp.maximum(q, 0)
            used = flag(q >= 0)
            outs[o - 1][n * SD : (n + 1) * SD, :] = source[segment(at), :] * used
            if info:
                outs[o - 1][NEAR + n : NEAR + n + 1, :] = source[pl.ds(FAR + at, 1), :] * used


def collect(route, replies, out):
    for q in range(SEG):
        o, n = lax.div(route[q], CAP), lax.rem(route[q], CAP)
        value = replies[1][segment(n), :]
        for w in (0, 2):
            value = jnp.where(o == w + 1, replies[w][segment(n), :], value)
        out[q * SD : (q + 1) * SD, :] = value


def fetch(place, near, far, k):
    seat = place[k]
    here = near[segment(jnp.minimum(seat, CAP - 1)), :]
    there = far[segment(jnp.maximum(seat - CAP, 0)), :]
    return jnp.where(seat < CAP, here, there)


def relay_kernel(far, pg, token, out1, out2, out3, inverse, info, sem):
    copy = pltpu.make_async_copy(far.at[pl.ds(FAR, SEG), :], info, sem)
    copy.start()
    copy.wait()
    outs = (out1, out2, out3)
    read_route(info, 0, None, inverse)
    spread(far, inverse, outs, True)
    out1[NEAR + CAP : NEAR + CAP + SEG, :] = far[FAR:, :]
    outs[HOP][NEAR + CAP :, :] = pg[...]


def exchange_kernel(
    route, inverse, near_source, far, r1, r2, r3, u, mask, token,
    f1, f2, f3, back, near,
):
    spread(far, inverse, (f1, f2, f3), False)
    f2[NEAR:, :] = u[RIGHT:, :]
    collect(route, (r1, r2, r3), back)
    for n in range(CAP):
        k = near_source[n]
        at = jnp.maximum(k, 0)
        near[n * SD : (n + 1) * SD, :] = u[rows(G + at * SD, SD), :] * mask[segment(at), :] * flag(k >= 0)


def select_kernel(near, u, token, s0, s1, s2, s3, info, sem):
    copy = pltpu.make_async_copy(near.at[pl.ds(CR, 8), :], info, sem)
    copy.start()
    copy.wait()
    for o, out in enumerate((s0, s1, s2, s3)):
        for n in range(CAP):
            j = info[0, o * CAP + n].astype(jnp.int32)
            out[n * SD : (n + 1) * SD, :] = near[segment(j), :]
    s2[NEAR:, :] = u[:G, :]


def split_kernel(
    near_source, position, slot, c_any, pc, pg, mortar, act_wide,
    high, low, partial, forth, back, near, both, tiles, sems,
):
    def fetch(i):
        return pltpu.make_async_copy(
            c_any.at[pl.ds(i * PIECE, PIECE), :], tiles.at[i % DEPTH], sems.at[i % DEPTH]
        )

    for i in range(DEPTH - 1):
        fetch(i).start()
    put_slots(near, near_source, CAP, pc, act_wide, slot, position)
    both[...] = jnp.zeros_like(both)
    for start, size, ref in ((G, CR, pc), (RIGHT, G, pg)):
        part_high, part_low = halves(ref[...])
        both[start : start + size, :LC] = part_high
        both[start : start + size, LC:] = part_low
    for j in range(SEG):
        block = mortar[j * SD : (j + 1) * SD, :]
        for ref, value in ((forth, -jnp.transpose(block)), (back, block)):
            part_high, part_low = halves(value)
            ref[2 * j * SD : (2 * j + 1) * SD, :] = part_high
            ref[(2 * j + 1) * SD : (2 * j + 2) * SD, :] = part_low
    for i in range(PIECES):
        if i + DEPTH - 1 < PIECES:
            fetch(i + DEPTH - 1).start()
        fetch(i).wait()
        at = slice(i * PIECE, (i + 1) * PIECE)
        part_high, part_low = halves(tiles[i % DEPTH])
        pad = jnp.zeros((PIECE, KP - NS), bf16)
        high[at, :NS] = part_high
        high[at, NS:] = pad
        low[at, :NS] = part_low
        low[at, NS:] = pad
        partial[at, :] = product(high[at, :], low[at, :], both[...])


def mortar_apply(mortar, j, value):
    part_high, part_low = halves(value)
    wide = jnp.concatenate([part_high, part_low], axis=1)
    parts = jnp.dot(mortar[2 * j * SD : (2 * j + 2) * SD, :], wide, preferred_element_type=f32)
    return (parts[SD:, LC:] + parts[SD:, :LC]) + parts[:SD, LC:] + parts[:SD, :LC]


def column_sum(value):
    return jnp.sum(value, axis=0, keepdims=True)


def first_kernel(
    me, in0, in1, in2, in3, forth, back, pc, pg, partial, mask, source, high, low,
    far, p0, p1, p2, p3, u, projected, actives, slots, route, inverse, sums,
    gathered, term, both, info, info_sems,
):
    ins = (in0, in1, in2, in3)
    infos = []
    for o in range(W):
        copy = pltpu.make_async_copy(ins[o].at[pl.ds(NEAR, 8), :], info.at[pl.ds(o * 8, 8), :], info_sems.at[o])
        copy.start()
        infos.append(copy)
    gathered[...] = jnp.zeros_like(gathered)
    actives[...] = jnp.zeros_like(actives)
    both[...] = jnp.zeros_like(both)
    left = -ins[HOP + 1][NEAR + CAP :, :] * flag(me[0] > 0)
    part_high, part_low = halves(left)
    both[:G, :LC] = part_high
    both[:G, LC:] = part_low
    copy = pltpu.make_async_copy(
        in1.at[pl.ds(NEAR + CAP, SEG), :], info.at[pl.ds(W * 8, SEG), :], info_sems.at[W]
    )
    copy.start()
    infos.append(copy)
    for copy in infos:
        copy.wait()
    read_route(info, W * 8, route, inverse)
    for o in range(W):
        tile = jnp.concatenate([ins[o][NEAR : NEAR + 8, :], jnp.zeros((120, 128), f32)], axis=0)
        columns = jnp.transpose(tile)
        for n in range(CAP):
            j = info[o * 8 + n, SD].astype(jnp.int32) - 1
            slots[o * CAP + n] = j
            at = rows(jnp.maximum(j, 0) * SD, SD)
            gathered[at, :] += ins[o][n * SD : (n + 1) * SD, :]
            actives[at, :] += jnp.broadcast_to(columns[:SD, n : n + 1], (SD, LC))
    for j in range(SEG):
        value = mortar_apply(forth, j, gathered[j * SD : (j + 1) * SD, :])
        term[j * SD : (j + 1) * SD, :] = value
        part_high, part_low = halves(value)
        start = K_LEFT + MASTER - K_LOW + j * SD
        both[start : start + SD, :LC] = part_high
        both[start : start + SD, LC:] = part_low
    for i in range(TILES):
        at = slice(i * TILE, (i + 1) * TILE)
        wide = slice(K_LOW, K_LOW + K_WIDE)
        u[at, :] = (
            partial[at, :]
            + product(high[at, :K_LEFT], low[at, :K_LEFT], both[:K_LEFT, :])
            + product(high[at, wide], low[at, wide], both[K_LEFT:, :])
        )
    p2[NEAR:, :] = u[:G, :]
    for j in range(SEG):
        start = MASTER + j * SD
        projected[j * SD : (j + 1) * SD, :] = mortar_apply(back, j, u[start : start + SD, :])
    for q in range(SEG):
        k = source[q]
        at = jnp.maximum(k, 0)
        far[q * SD : (q + 1) * SD, :] = u[rows(G + at * SD, SD), :] * mask[segment(at), :] * flag(k >= 0)
    for o, reply in enumerate((p0, p1, p2, p3)):
        for n in range(CAP):
            j = jnp.maximum(slots[o * CAP + n], 0)
            reply[n * SD : (n + 1) * SD, :] = projected[segment(j), :]
    norm = column_sum(pg[...] * pg[...]) + column_sum(pc[...] * pc[...])
    curvature = (
        column_sum(pg[...] * u[RIGHT:, :])
        + column_sum(left * u[:G, :])
        + column_sum(pc[...] * u[G:MASTER, :])
        + column_sum(term[...] * u[MASTER:RIGHT, :])
    )
    sums[...] = jnp.concatenate([norm, curvature, jnp.zeros((6, LC), f32)], axis=0)


def master_kernel(
    slots, f0, f1, f2, f3, projected0, actives, forth, high, low, partial, term, gathered, both
):
    gathered[...] = -(actives[...] * projected0[...])
    for o, source in enumerate((f0, f1, f2, f3)):
        for n in range(CAP):
            at = segment(jnp.maximum(slots[o * CAP + n], 0))
            gathered[at, :] += source[n * SD : (n + 1) * SD, :]
    both[...] = jnp.zeros_like(both)
    for j in range(SEG):
        value = mortar_apply(forth, j, gathered[j * SD : (j + 1) * SD, :])
        term[j * SD : (j + 1) * SD, :] = value
        part_high, part_low = halves(value)
        start = MASTER - K_LOW + j * SD
        both[start : start + SD, :LC] = part_high
        both[start : start + SD, LC:] = part_low
    wide = slice(K_LOW, K_LOW + K_WIDE)
    for i in range(TILES):
        at = slice(i * TILE, (i + 1) * TILE)
        partial[at, :] = product(high[at, wide], low[at, wide], both[...])


def second_kernel(
    me, place, near, far, r2, f2, u0, mask, partial, term, sums0, high, low,
    u, q_glue, q_contact, sums,
    loads, both,
):
    loads[:G, :] = (u0[:G, :] - f2[NEAR:, :]) * flag(me[0] > 0)
    glue = u0[RIGHT:, :] - r2[NEAR:, :] * flag(me[0] < NSUB - 1)
    q_glue[...] = glue
    for k in range(SEG):
        here = slice(k * SD, (k + 1) * SD)
        fetched = fetch(place, near, far, k)
        value = mask[here, :] * (u0[G + k * SD : G + (k + 1) * SD, :] - fetched)
        q_contact[here, :] = value
        loads[G + k * SD : G + (k + 1) * SD, :] = value
    loads[MASTER:K_NEAR, :] = jnp.zeros((K_NEAR - MASTER, LC), f32)
    both[K_NEAR:, :] = jnp.zeros((K_PAD, 2 * LC), bf16)
    start = K_NEAR + RIGHT - K_RIGHT
    for at, value in ((slice(0, K_NEAR), loads[...]), (slice(start, start + G), glue)):
        part_high, part_low = halves(value)
        both[at, :LC] = part_high
        both[at, LC:] = part_low
    tail = slice(K_RIGHT, K_RIGHT + K_PAD)
    for i in range(TILES):
        at = slice(i * TILE, (i + 1) * TILE)
        u[at, :] = (
            partial[at, :]
            + product(high[at, :K_NEAR], low[at, :K_NEAR], both[:K_NEAR, :])
            + product(high[at, tail], low[at, tail], both[K_NEAR:, :])
        )
    square = column_sum(glue * glue) + column_sum(q_contact[...] * q_contact[...])
    energy = (
        column_sum(loads[:MASTER, :] * u[:MASTER, :])
        + column_sum(term[...] * u[MASTER:RIGHT, :])
        + column_sum(glue * u[RIGHT:, :])
    )
    sums[...] = jnp.concatenate([sums0[0:2, :], square, energy, jnp.zeros((4, LC), f32)], axis=0)


def reply_kernel(slots, project, u, sums, out, kept):
    kept[...] = sums[...]
    for j in range(SEG):
        start = MASTER + j * SD
        out[j * SD : (j + 1) * SD, :] = mortar_apply(project, j, u[start : start + SD, :])
    lane = lax.broadcasted_iota(jnp.int32, (8, 128), 1)
    row = jnp.zeros((8, 128), f32)
    for i in range(SLOTS):
        row = jnp.where(lane == i, jnp.maximum(slots[i], 0).astype(f32), row)
    out[CR:, :] = row


def last_kernel(
    me, position, s0, s1, s2, s3, u, q_glue, q_contact, pc, pg, mask, sums,
    mult_glue, mult_contact, res_glue, res_contact,
):
    norm0, curvature0, square, energy = (sums[i : i + 1, :] for i in range(4))
    alpha0 = norm0 / curvature0
    norm1 = (norm0 - alpha0 * curvature0) + alpha0 * (alpha0 * square - curvature0)
    own = (curvature0 - alpha0 * square) + alpha0 * (alpha0 * energy - square)
    cross = curvature0 - alpha0 * square
    ratio = norm1 / norm0
    curvature1 = own + ratio * (2.0 * cross + ratio * curvature0)
    alpha1 = norm1 / curvature1

    def finish(r0, q, w):
        r1 = r0 - alpha0 * q
        direction = r1 + ratio * r0
        image = (q - alpha0 * w) + ratio * q
        return alpha0 * r0 + alpha1 * direction, r1 - alpha1 * image

    mult, res = finish(pg[...], q_glue[...], u[RIGHT:, :] - s2[NEAR:, :] * flag(me[0] < NSUB - 1))
    mult_glue[...] = mult
    res_glue[...] = res
    for k in range(SEG):
        here = slice(k * SD, (k + 1) * SD)
        o, n = lax.div(position[k], CAP), lax.rem(position[k], CAP)
        fetched = s0[segment(n), :]
        for w, ref in ((1, s1), (2, s2), (3, s3)):
            fetched = jnp.where(o == w, ref[segment(n), :], fetched)
        value = mask[here, :] * (u[G + k * SD : G + (k + 1) * SD, :] - fetched)
        mult, res = finish(pc[here, :], q_contact[here, :], value)
        mult_contact[here, :] = mult
        res_contact[here, :] = res


def shape(*dims, dtype=f32):
    return jax.ShapeDtypeStruct(dims, dtype)


def params(mib):
    return pltpu.CompilerParams(vmem_limit_bytes=mib * MIB)


def sent(value, body_step, sub_step):
    subs, bodies = lax.axis_size("sub"), lax.axis_size("body")
    pairs = [
        (s * bodies + b, ((s + sub_step) % subs) * bodies + (b + body_step) % bodies)
        for s in range(subs)
        for b in range(bodies)
    ]
    return lax.ppermute(value, ("sub", "body"), pairs)


def moved(value, body_step, sub_step):
    return sent(value, body_step, sub_step) if body_step or sub_step else value


def rotated(value, block, stride, steps):
    count = lax.axis_size("sub")
    pairs = []
    for s in range(count):
        place = s // stride % block
        pairs.append((s, s + ((place + steps) % block - place) * stride))
    return lax.ppermute(value, "sub", pairs)


def total(value):
    value = value + sum(rotated(value, 4, 2, k) for k in (1, 2, 3))
    value = value + rotated(value, 2, 1, 1)
    token = value
    value = value + sum(rotated(value, 4, 8, k) for k in (1, 2, 3))
    value = value + sent(value, 1, 0) + sent(value, 2, 0) + sent(value, 3, 0)
    return value, token


def in_hbm(value):
    return pltpu.with_memory_space_constraint(value, pltpu.HBM)


def kept(value):
    return pltpu.with_memory_space_constraint(value, pltpu.VMEM)


def per_device(compliance, mortar, rhs_glue, rhs_contact, owner_sub, master_slot, active_set):
    schur_block = compliance[0, 0]
    blocks = mortar.reshape(CR, SD)
    rhs = rhs_contact.reshape(CR, LC)
    me = lax.axis_index("sub").astype(jnp.int32).reshape(1)
    seg_block = shape(NEAR, LC)
    far_block = shape(FAR, LC)
    info_block = shape(NEAR + CAP, LC)
    face_block = shape(NEAR + G, LC)

    def index(n):
        return shape(n, dtype=jnp.int32)

    far, pc, mask, pg, act_wide, near_source, far_source, place, position, slot = pl.pallas_call(
        pack_kernel,
        out_shape=[shape(FAR + SEG, LC), shape(CR, LC), shape(CR, LC), shape(G, LC), shape(SEG, 128)]
        + [index(n) for n in (CAP, SEG, SEG, SEG, SEG)],
        in_specs=[SM] + [ANY] * 5,
        out_specs=[VM] * 5 + [SM] * 5,
        scratch_shapes=[
            pltpu.SMEM((SEG,), jnp.int32),
            pltpu.VMEM((SEG, SD), jnp.int32),
            pltpu.VMEM((CR, LC), f32),
            pltpu.SMEM((W + 1,), jnp.int32),
            pltpu.SemaphoreType.DMA((5,)),
        ],
        compiler_params=params(8),
        name="pack",
    )(me, *(in_hbm(v) for v in (
        owner_sub.reshape(SEG), master_slot.reshape(SEG), active_set.reshape(SEG, SD), rhs, rhs_glue[0, 0],
    )))

    far_in = sent(far, 1, HOP)

    stacked = shape(2 * CR, SD, dtype=bf16)
    high, low, partial, forth, project, near = pl.pallas_call(
        split_kernel,
        out_shape=[pltpu.VMEM((NS, KP), bf16)] * 2 + [shape(NS, LC), stacked, stacked, info_block],
        in_specs=[SM] * 3 + [ANY] + [VM] * 4,
        out_specs=[VM] * 6,
        scratch_shapes=[
            pltpu.VMEM((KP, 2 * LC), bf16),
            pltpu.VMEM((DEPTH, PIECE, NS), f32),
            pltpu.SemaphoreType.DMA((DEPTH,)),
        ],
        compiler_params=params(20),
        cost_estimate=pl.CostEstimate(
            flops=8 * NS * KP * LC, bytes_accessed=4 * NS * NS, transcendentals=0
        ),
        name="split",
    )(near_source, position, slot, in_hbm(schur_block), pc, pg, blocks, act_wide)
    high, low = kept(high), kept(low)
    near_in = sent(near, 1, 0)

    relayed = [shape(NEAR + CAP + extra, LC) for extra in ((SEG, 0, G) if HOP == 2 else (SEG, G, 0))]
    outgoing = pl.pallas_call(
        relay_kernel,
        out_shape=relayed + [index(SLOTS)],
        in_specs=[VM, VM, ANY],
        out_specs=[VM] * 3 + [SM],
        scratch_shapes=[pltpu.SMEM((SEG, 128), f32), pltpu.SemaphoreType.DMA],
        compiler_params=params(6),
        name="relay",
    )(far_in, pg, partial)
    incoming = [near_in] + [moved(outgoing[o - 1], 0, o - HOP) for o in range(1, W)]

    outs = pl.pallas_call(
        first_kernel,
        out_shape=[far_block, seg_block, seg_block, face_block, seg_block]
        + [shape(NS, LC), shape(CR, LC), shape(CR, LC)]
        + [index(SLOTS), index(SEG), index(SLOTS), shape(8, LC)],
        in_specs=[SM] + [VM] * 10 + [SM, VM, VM],
        out_specs=[VM] * 8 + [SM] * 3 + [VM],
        scratch_shapes=[
            pltpu.VMEM((CR, LC), f32),
            pltpu.VMEM((CR, LC), f32),
            pltpu.VMEM((K_LEFT + K_WIDE, 2 * LC), bf16),
            pltpu.SMEM((W * 8 + SEG, 128), f32),
            pltpu.SemaphoreType.DMA((W + 1,)),
        ],
        compiler_params=params(12),
        name="first",
    )(me, *incoming, forth, project, pc, pg, partial, mask, far_source, high, low)
    far, replies = outs[0], outs[1:5]
    u0, projected0, actives, slots, route, inverse, sums0 = outs[5:]

    far_in = sent(far, 1, BACK_HOP)
    replies = [sent(replies[0], -1, 0)] + [moved(replies[o], 0, BACK_HOP - o) for o in range(1, W)]
    near_back, next_left = replies[0], replies[2]

    *outgoing, far, near = pl.pallas_call(
        exchange_kernel,
        out_shape=[seg_block, face_block, seg_block, far_block, seg_block],
        in_specs=[SM] * 3 + [VM] * 6 + [ANY],
        out_specs=[VM] * 5,
        compiler_params=params(12),
        name="exchange",
    )(route, inverse, near_source, far_in, *replies[1:], u0, mask, near_back)
    far_back = sent(far, -1, -BACK_HOP)
    incoming = [sent(near, 1, 0)] + [moved(outgoing[o - 1], 0, o - BACK_HOP) for o in range(1, W)]

    partial, term = pl.pallas_call(
        master_kernel,
        out_shape=[shape(NS, LC), shape(CR, LC)],
        in_specs=[SM] + [VM] * 9,
        out_specs=[VM] * 2,
        scratch_shapes=[pltpu.VMEM((CR, LC), f32), pltpu.VMEM((K_WIDE, 2 * LC), bf16)],
        compiler_params=params(12),
        cost_estimate=pl.CostEstimate(flops=8 * NS * K_WIDE * LC, bytes_accessed=MIB, transcendentals=0),
        name="master",
    )(slots, *incoming, projected0, actives, forth, high, low)

    u1, q_glue, q_contact, sums = pl.pallas_call(
        second_kernel,
        out_shape=[shape(NS, LC), shape(G, LC), shape(CR, LC), shape(8, LC)],
        in_specs=[SM] * 2 + [VM] * 11,
        out_specs=[VM] * 4,
        scratch_shapes=[pltpu.VMEM((K_NEAR, LC), f32), pltpu.VMEM((K_NEAR + K_PAD, 2 * LC), bf16)],
        compiler_params=params(12),
        name="second",
    )(me, place, near_back, far_back, next_left, incoming[2], u0, mask, partial, term, sums0, high, low)

    replied, sums = pl.pallas_call(
        reply_kernel,
        out_shape=[shape(CR + 8, LC), shape(8, LC)],
        in_specs=[SM] + [VM] * 3,
        out_specs=[VM] * 2,
        compiler_params=params(8),
        cost_estimate=pl.CostEstimate(flops=0, bytes_accessed=8 * MIB, transcendentals=0),
        name="reply",
    )(slots, project, u1, sums)
    replied = sent(replied, -1, -1)
    sums, token = total(sums)

    *outgoing, = pl.pallas_call(
        select_kernel,
        out_shape=[seg_block, seg_block, face_block, seg_block],
        in_specs=[VM] * 2 + [ANY],
        out_specs=[VM] * 4,
        scratch_shapes=[pltpu.SMEM((8, 128), f32), pltpu.SemaphoreType.DMA],
        compiler_params=params(6),
        name="select",
    )(replied, u1, token)
    fetched = [moved(outgoing[o], 0, 1 - o) for o in range(W)]

    mult_glue, mult_contact, res_glue, res_contact = pl.pallas_call(
        last_kernel,
        out_shape=[shape(G, LC), shape(CR, LC)] * 2,
        in_specs=[SM] * 2 + [VM] * 11,
        out_specs=[VM] * 4,
        compiler_params=params(24),
        name="last",
    )(me, position, *fetched, u1, q_glue, q_contact, pc, pg, mask, sums)
    contact = (1, 1, SEG, SD, LC)
    return (
        mult_glue[None, None],
        mult_contact.reshape(contact),
        res_glue[None, None],
        res_contact.reshape(contact),
    )


def solution(mesh):
    in_specs = (
        P("body", "sub", None, None),
        P("body", "sub", None, None, None),
        P("body", "sub", None, None),
        P("body", "sub", None, None, None),
        P("body", "sub", None, None),
        P("body", "sub", None),
        P("body", "sub", None, None),
    )
    out_specs = (
        P("body", "sub", None, None),
        P("body", "sub", None, None, None),
        P("body", "sub", None, None),
        P("body", "sub", None, None, None),
    )
    return jax.shard_map(
        per_device, mesh=mesh, in_specs=in_specs, out_specs=out_specs, check_vma=False
    )
```

```python
import jax
import jax.numpy as jnp
from jax import lax
from jax.experimental import pallas as pl
from jax.experimental.pallas import tpu as pltpu
from jax.sharding import PartitionSpec as P

W = 4
CAP = 8
SLOTS = W * CAP
SEG = 16
SD = 64
LC = 128
G = 176
NS = 2400
CR = SEG * SD
MASTER = G + CR
RIGHT = G + 2 * CR
KP = 2560
K_LOW, K_WIDE = 1152, 1152
K_LEFT = 256
K_NEAR = 1280
K_RIGHT = 2176
K_PAD = 256
HOP = 1
PAD = 200
BACK_HOP = 1
TILE = 240
TILES = NS // TILE
PIECE = 240
PIECES = NS // PIECE
DEPTH = 4
NEAR = CAP * SD
FAR = SEG * SD
NSUB = 32
MIB = 1 << 20

f32 = jnp.float32
bf16 = jnp.bfloat16
highest = lax.Precision.HIGHEST
VM = pl.BlockSpec(memory_space=pltpu.VMEM)
SM = pl.BlockSpec(memory_space=pltpu.SMEM)
ANY = pl.BlockSpec(memory_space=pl.ANY)


def rows(start, size):
    return pl.ds(pl.multiple_of(start, 8), size)


def halves(value):
    high = value.astype(bf16)
    low = (value - high.astype(f32)).astype(bf16)
    return high, low


def product(high, low, both):
    first = jnp.dot(high, both, preferred_element_type=f32)
    second = jnp.dot(low, both, preferred_element_type=f32)
    return (first[:, LC:] + second[:, LC:]) + second[:, :LC] + first[:, :LC]


def segment(index):
    return pl.ds(pl.multiple_of(index * SD, SD), SD)


def flag(condition):
    return jnp.where(condition, 1.0, 0.0).astype(f32)


def put_slots(ref, source, slots, pc, act_wide, slot, position):
    lane = lax.broadcasted_iota(jnp.int32, (1, 128), 1)
    for n in range(slots):
        k = source[n]
        at = jnp.maximum(k, 0)
        used = flag(k >= 0)
        ref[n * SD : (n + 1) * SD, :] = pc[segment(at), :] * used
        tag = (slot[at] + 1).astype(f32)
        seat = position[at].astype(f32)
        row = jnp.where(lane == SD, tag, jnp.where(lane == SD + 1, seat, act_wide[pl.ds(at, 1), :]))
        ref[slots * SD + n : slots * SD + n + 1, :] = used * row


def pack_kernel(
    me, owner_any, slot_any, act_any, rhs_any, glue_any,
    far, pc, mask, pg, act_wide, near_source, far_source, place, position, slot,
    owner, act, rhs, count, sems,
):
    pairs = ((owner_any, owner), (slot_any, slot), (act_any, act), (rhs_any, rhs), (glue_any, pg))
    copies = [pltpu.make_async_copy(src, dst, sems.at[i]) for i, (src, dst) in enumerate(pairs)]
    for copy in copies:
        copy.start()
    for i in range(SEG):
        far_source[i] = -1
    for n in range(CAP):
        near_source[n] = -1
    for o in range(W + 1):
        count[o] = 0
    copies[0].wait()
    for k in range(SEG):
        o = lax.rem(owner[k] - me[0] + NSUB, NSUB)
        n = count[o]
        q = count[W]
        count[o] = n + 1
        position[k] = o * CAP + n

        @pl.when(o == 0)
        def _():
            near_source[n] = k
            place[k] = n

        @pl.when(o > 0)
        def _():
            far_source[q] = k
            place[k] = CAP + q
            count[W] = q + 1

    for copy in copies[1:]:
        copy.wait()
    active = act[...].astype(f32)
    act_wide[...] = jnp.concatenate([active, jnp.zeros((SEG, 128 - SD), f32)], axis=1)
    columns = jnp.transpose(jnp.concatenate([act_wide[...], jnp.zeros((128 - SEG, 128), f32)], axis=0))
    for k in range(SEG):
        wide = jnp.broadcast_to(columns[:SD, k : k + 1], (SD, LC))
        here = slice(k * SD, (k + 1) * SD)
        mask[here, :] = wide
        pc[here, :] = rhs[here, :] * wide
    put_slots(far, far_source, SEG, pc, act_wide, slot, position)


def read_route(info, first, route, inverse):
    for i in range(SLOTS):
        inverse[i] = -1
    for q in range(SEG):
        seat = info[first + q, SD + 1].astype(jnp.int32)
        if route is not None:
            route[q] = seat

        @pl.when(seat > 0)
        def _():
            inverse[seat] = q


def spread(source, inverse, outs, info):
    for o in range(1, W):
        for n in range(CAP):
            q = inverse[o * CAP + n]
            at = jnp.maximum(q, 0)
            used = flag(q >= 0)
            outs[o - 1][n * SD : (n + 1) * SD, :] = source[segment(at), :] * used
            if info:
                outs[o - 1][NEAR + n : NEAR + n + 1, :] = source[pl.ds(FAR + at, 1), :] * used


def collect(route, replies, out):
    for q in range(SEG):
        o, n = lax.div(route[q], CAP), lax.rem(route[q], CAP)
        value = replies[1][segment(n), :]
        for w in (0, 2):
            value = jnp.where(o == w + 1, replies[w][segment(n), :], value)
        out[q * SD : (q + 1) * SD, :] = value


def fetch(place, near, far, k):
    seat = place[k]
    here = near[segment(jnp.minimum(seat, CAP - 1)), :]
    there = far[segment(jnp.maximum(seat - CAP, 0)), :]
    return jnp.where(seat < CAP, here, there)


def relay_kernel(far, pg, token, out1, out2, out3, inverse, info, sem):
    copy = pltpu.make_async_copy(far.at[pl.ds(FAR, SEG), :], info, sem)
    copy.start()
    copy.wait()
    outs = (out1, out2, out3)
    read_route(info, 0, None, inverse)
    spread(far, inverse, outs, True)
    out1[NEAR + CAP : NEAR + CAP + SEG, :] = far[FAR:, :]
    outs[HOP][NEAR + CAP :, :] = pg[...]


def exchange_kernel(
    route, inverse, near_source, far, r1, r2, r3, u, mask, token,
    f1, f2, f3, back, near,
):
    spread(far, inverse, (f1, f2, f3), False)
    f2[NEAR:, :] = u[RIGHT:, :]
    collect(route, (r1, r2, r3), back)
    for n in range(CAP):
        k = near_source[n]
        at = jnp.maximum(k, 0)
        near[n * SD : (n + 1) * SD, :] = u[rows(G + at * SD, SD), :] * mask[segment(at), :] * flag(k >= 0)


def select_kernel(near, u, token, s0, s1, s2, s3, info, sem):
    copy = pltpu.make_async_copy(near.at[pl.ds(CR, 8), :], info, sem)
    copy.start()
    copy.wait()
    for o, out in enumerate((s0, s1, s2, s3)):
        for n in range(CAP):
            j = info[0, o * CAP + n].astype(jnp.int32)
            out[n * SD : (n + 1) * SD, :] = near[segment(j), :]
    s2[NEAR:, :] = u[:G, :]


def split_kernel(
    near_source, position, slot, c_any, pc, pg, mortar, act_wide,
    high, low, partial, forth, back, near, both, tiles, sems,
):
    def fetch(i):
        return pltpu.make_async_copy(
            c_any.at[pl.ds(i * PIECE, PIECE), :], tiles.at[i % DEPTH], sems.at[i % DEPTH]
        )

    for i in range(DEPTH - 1):
        fetch(i).start()
    put_slots(near, near_source, CAP, pc, act_wide, slot, position)
    near[NEAR + CAP :, :] = jnp.zeros((PAD, LC), f32)
    both[...] = jnp.zeros_like(both)
    for start, size, ref in ((G, CR, pc), (RIGHT, G, pg)):
        part_high, part_low = halves(ref[...])
        both[start : start + size, :LC] = part_high
        both[start : start + size, LC:] = part_low
    for j in range(SEG):
        block = mortar[j * SD : (j + 1) * SD, :]
        for ref, value in ((forth, -jnp.transpose(block)), (back, block)):
            part_high, part_low = halves(value)
            ref[2 * j * SD : (2 * j + 1) * SD, :] = part_high
            ref[(2 * j + 1) * SD : (2 * j + 2) * SD, :] = part_low
    for i in range(PIECES):
        if i + DEPTH - 1 < PIECES:
            fetch(i + DEPTH - 1).start()
        fetch(i).wait()
        at = slice(i * PIECE, (i + 1) * PIECE)
        part_high, part_low = halves(tiles[i % DEPTH])
        pad = jnp.zeros((PIECE, KP - NS), bf16)
        high[at, :NS] = part_high
        high[at, NS:] = pad
        low[at, :NS] = part_low
        low[at, NS:] = pad
        partial[at, :] = product(high[at, :], low[at, :], both[...])


def mortar_apply(mortar, j, value):
    part_high, part_low = halves(value)
    wide = jnp.concatenate([part_high, part_low], axis=1)
    parts = jnp.dot(mortar[2 * j * SD : (2 * j + 2) * SD, :], wide, preferred_element_type=f32)
    return (parts[SD:, LC:] + parts[SD:, :LC]) + parts[:SD, LC:] + parts[:SD, :LC]


def column_sum(value):
    return jnp.sum(value, axis=0, keepdims=True)


def first_kernel(
    me, in0, in1, in2, in3, forth, back, pc, pg, partial, mask, source, high, low,
    far, p0, p1, p2, p3, u, projected, actives, slots, route, inverse, sums,
    gathered, term, both, info, info_sems,
):
    ins = (in0, in1, in2, in3)
    infos = []
    for o in range(W):
        copy = pltpu.make_async_copy(ins[o].at[pl.ds(NEAR, 8), :], info.at[pl.ds(o * 8, 8), :], info_sems.at[o])
        copy.start()
        infos.append(copy)
    gathered[...] = jnp.zeros_like(gathered)
    actives[...] = jnp.zeros_like(actives)
    both[...] = jnp.zeros_like(both)
    left = -ins[HOP + 1][NEAR + CAP :, :] * flag(me[0] > 0)
    part_high, part_low = halves(left)
    both[:G, :LC] = part_high
    both[:G, LC:] = part_low
    copy = pltpu.make_async_copy(
        in1.at[pl.ds(NEAR + CAP, SEG), :], info.at[pl.ds(W * 8, SEG), :], info_sems.at[W]
    )
    copy.start()
    infos.append(copy)
    for copy in infos:
        copy.wait()
    read_route(info, W * 8, route, inverse)
    for o in range(W):
        tile = jnp.concatenate([ins[o][NEAR : NEAR + 8, :], jnp.zeros((120, 128), f32)], axis=0)
        columns = jnp.transpose(tile)
        for n in range(CAP):
            j = info[o * 8 + n, SD].astype(jnp.int32) - 1
            slots[o * CAP + n] = j
            at = rows(jnp.maximum(j, 0) * SD, SD)
            gathered[at, :] += ins[o][n * SD : (n + 1) * SD, :]
            actives[at, :] += jnp.broadcast_to(columns[:SD, n : n + 1], (SD, LC))
    for j in range(SEG):
        value = mortar_apply(forth, j, gathered[j * SD : (j + 1) * SD, :])
        term[j * SD : (j + 1) * SD, :] = value
        part_high, part_low = halves(value)
        start = K_LEFT + MASTER - K_LOW + j * SD
        both[start : start + SD, :LC] = part_high
        both[start : start + SD, LC:] = part_low
    for i in range(TILES):
        at = slice(i * TILE, (i + 1) * TILE)
        wide = slice(K_LOW, K_LOW + K_WIDE)
        u[at, :] = (
            partial[at, :]
            + product(high[at, :K_LEFT], low[at, :K_LEFT], both[:K_LEFT, :])
            + product(high[at, wide], low[at, wide], both[K_LEFT:, :])
        )
    p2[NEAR:, :] = u[:G, :]
    for j in range(SEG):
        start = MASTER + j * SD
        projected[j * SD : (j + 1) * SD, :] = mortar_apply(back, j, u[start : start + SD, :])
    for q in range(SEG):
        k = source[q]
        at = jnp.maximum(k, 0)
        far[q * SD : (q + 1) * SD, :] = u[rows(G + at * SD, SD), :] * mask[segment(at), :] * flag(k >= 0)
    for o, reply in enumerate((p0, p1, p2, p3)):
        for n in range(CAP):
            j = jnp.maximum(slots[o * CAP + n], 0)
            reply[n * SD : (n + 1) * SD, :] = projected[segment(j), :]
    norm = column_sum(pg[...] * pg[...]) + column_sum(pc[...] * pc[...])
    curvature = (
        column_sum(pg[...] * u[RIGHT:, :])
        + column_sum(left * u[:G, :])
        + column_sum(pc[...] * u[G:MASTER, :])
        + column_sum(term[...] * u[MASTER:RIGHT, :])
    )
    sums[...] = jnp.concatenate([norm, curvature, jnp.zeros((6, LC), f32)], axis=0)


def master_kernel(
    slots, f0, f1, f2, f3, projected0, actives, forth, high, low, partial, term, gathered, both
):
    gathered[...] = -(actives[...] * projected0[...])
    for o, source in enumerate((f0, f1, f2, f3)):
        for n in range(CAP):
            at = segment(jnp.maximum(slots[o * CAP + n], 0))
            gathered[at, :] += source[n * SD : (n + 1) * SD, :]
    both[...] = jnp.zeros_like(both)
    for j in range(SEG):
        value = mortar_apply(forth, j, gathered[j * SD : (j + 1) * SD, :])
        term[j * SD : (j + 1) * SD, :] = value
        part_high, part_low = halves(value)
        start = MASTER - K_LOW + j * SD
        both[start : start + SD, :LC] = part_high
        both[start : start + SD, LC:] = part_low
    wide = slice(K_LOW, K_LOW + K_WIDE)
    for i in range(TILES):
        at = slice(i * TILE, (i + 1) * TILE)
        partial[at, :] = product(high[at, wide], low[at, wide], both[...])


def second_kernel(
    me, place, near, far, r2, f2, u0, mask, partial, term, sums0, high, low,
    u, q_glue, q_contact, sums,
    loads, both,
):
    loads[:G, :] = (u0[:G, :] - f2[NEAR:, :]) * flag(me[0] > 0)
    glue = u0[RIGHT:, :] - r2[NEAR:, :] * flag(me[0] < NSUB - 1)
    q_glue[...] = glue
    for k in range(SEG):
        here = slice(k * SD, (k + 1) * SD)
        fetched = fetch(place, near, far, k)
        value = mask[here, :] * (u0[G + k * SD : G + (k + 1) * SD, :] - fetched)
        q_contact[here, :] = value
        loads[G + k * SD : G + (k + 1) * SD, :] = value
    loads[MASTER:K_NEAR, :] = jnp.zeros((K_NEAR - MASTER, LC), f32)
    both[K_NEAR:, :] = jnp.zeros((K_PAD, 2 * LC), bf16)
    start = K_NEAR + RIGHT - K_RIGHT
    for at, value in ((slice(0, K_NEAR), loads[...]), (slice(start, start + G), glue)):
        part_high, part_low = halves(value)
        both[at, :LC] = part_high
        both[at, LC:] = part_low
    tail = slice(K_RIGHT, K_RIGHT + K_PAD)
    for i in range(TILES):
        at = slice(i * TILE, (i + 1) * TILE)
        u[at, :] = (
            partial[at, :]
            + product(high[at, :K_NEAR], low[at, :K_NEAR], both[:K_NEAR, :])
            + product(high[at, tail], low[at, tail], both[K_NEAR:, :])
        )
    square = column_sum(glue * glue) + column_sum(q_contact[...] * q_contact[...])
    energy = (
        column_sum(loads[:MASTER, :] * u[:MASTER, :])
        + column_sum(term[...] * u[MASTER:RIGHT, :])
        + column_sum(glue * u[RIGHT:, :])
    )
    sums[...] = jnp.concatenate([sums0[0:2, :], square, energy, jnp.zeros((4, LC), f32)], axis=0)


def reply_kernel(slots, project, u, sums, out, kept):
    kept[...] = sums[...]
    for j in range(SEG):
        start = MASTER + j * SD
        out[j * SD : (j + 1) * SD, :] = mortar_apply(project, j, u[start : start + SD, :])
    lane = lax.broadcasted_iota(jnp.int32, (8, 128), 1)
    row = jnp.zeros((8, 128), f32)
    for i in range(SLOTS):
        row = jnp.where(lane == i, jnp.maximum(slots[i], 0).astype(f32), row)
    out[CR:, :] = row


def last_kernel(
    me, position, s0, s1, s2, s3, u, q_glue, q_contact, pc, pg, mask, sums,
    mult_glue, mult_contact, res_glue, res_contact,
):
    norm0, curvature0, square, energy = (sums[i : i + 1, :] for i in range(4))
    alpha0 = norm0 / curvature0
    norm1 = (norm0 - alpha0 * curvature0) + alpha0 * (alpha0 * square - curvature0)
    own = (curvature0 - alpha0 * square) + alpha0 * (alpha0 * energy - square)
    cross = curvature0 - alpha0 * square
    ratio = norm1 / norm0
    curvature1 = own + ratio * (2.0 * cross + ratio * curvature0)
    alpha1 = norm1 / curvature1

    def finish(r0, q, w):
        r1 = r0 - alpha0 * q
        direction = r1 + ratio * r0
        image = (q - alpha0 * w) + ratio * q
        return alpha0 * r0 + alpha1 * direction, r1 - alpha1 * image

    mult, res = finish(pg[...], q_glue[...], u[RIGHT:, :] - s2[NEAR:, :] * flag(me[0] < NSUB - 1))
    mult_glue[...] = mult
    res_glue[...] = res
    for k in range(SEG):
        here = slice(k * SD, (k + 1) * SD)
        o, n = lax.div(position[k], CAP), lax.rem(position[k], CAP)
        fetched = s0[segment(n), :]
        for w, ref in ((1, s1), (2, s2), (3, s3)):
            fetched = jnp.where(o == w, ref[segment(n), :], fetched)
        value = mask[here, :] * (u[G + k * SD : G + (k + 1) * SD, :] - fetched)
        mult, res = finish(pc[here, :], q_contact[here, :], value)
        mult_contact[here, :] = mult
        res_contact[here, :] = res


def shape(*dims, dtype=f32):
    return jax.ShapeDtypeStruct(dims, dtype)


def params(mib):
    return pltpu.CompilerParams(vmem_limit_bytes=mib * MIB)


def sent(value, body_step, sub_step):
    subs, bodies = lax.axis_size("sub"), lax.axis_size("body")
    pairs = [
        (s * bodies + b, ((s + sub_step) % subs) * bodies + (b + body_step) % bodies)
        for s in range(subs)
        for b in range(bodies)
    ]
    return lax.ppermute(value, ("sub", "body"), pairs)


def moved(value, body_step, sub_step):
    return sent(value, body_step, sub_step) if body_step or sub_step else value


def rotated(value, block, stride, steps):
    count = lax.axis_size("sub")
    pairs = []
    for s in range(count):
        place = s // stride % block
        pairs.append((s, s + ((place + steps) % block - place) * stride))
    return lax.ppermute(value, "sub", pairs)


def total(value):
    value = value + sum(rotated(value, 4, 2, k) for k in (1, 2, 3))
    value = value + rotated(value, 2, 1, 1)
    token = value
    value = value + sum(rotated(value, 4, 8, k) for k in (1, 2, 3))
    value = value + sent(value, 1, 0) + sent(value, 2, 0) + sent(value, 3, 0)
    return value, token


def in_hbm(value):
    return pltpu.with_memory_space_constraint(value, pltpu.HBM)


def kept(value):
    return pltpu.with_memory_space_constraint(value, pltpu.VMEM)


def per_device(compliance, mortar, rhs_glue, rhs_contact, owner_sub, master_slot, active_set):
    schur_block = compliance[0, 0]
    blocks = mortar.reshape(CR, SD)
    rhs = rhs_contact.reshape(CR, LC)
    me = lax.axis_index("sub").astype(jnp.int32).reshape(1)
    seg_block = shape(NEAR, LC)
    far_block = shape(FAR, LC)
    info_block = shape(NEAR + CAP, LC)
    face_block = shape(NEAR + G, LC)

    def index(n):
        return shape(n, dtype=jnp.int32)

    far, pc, mask, pg, act_wide, near_source, far_source, place, position, slot = pl.pallas_call(
        pack_kernel,
        out_shape=[shape(FAR + SEG, LC), shape(CR, LC), shape(CR, LC), shape(G, LC), shape(SEG, 128)]
        + [index(n) for n in (CAP, SEG, SEG, SEG, SEG)],
        in_specs=[SM] + [ANY] * 5,
        out_specs=[VM] * 5 + [SM] * 5,
        scratch_shapes=[
            pltpu.SMEM((SEG,), jnp.int32),
            pltpu.VMEM((SEG, SD), jnp.int32),
            pltpu.VMEM((CR, LC), f32),
            pltpu.SMEM((W + 1,), jnp.int32),
            pltpu.SemaphoreType.DMA((5,)),
        ],
        compiler_params=params(8),
        name="pack",
    )(me, *(in_hbm(v) for v in (
        owner_sub.reshape(SEG), master_slot.reshape(SEG), active_set.reshape(SEG, SD), rhs, rhs_glue[0, 0],
    )))

    far_in = sent(far, 1, HOP)

    stacked = shape(2 * CR, SD, dtype=bf16)
    high, low, partial, forth, project, near = pl.pallas_call(
        split_kernel,
        out_shape=[pltpu.VMEM((NS, KP), bf16)] * 2 + [shape(NS, LC), stacked, stacked, shape(NEAR + CAP + PAD, LC)],
        in_specs=[SM] * 3 + [ANY] + [VM] * 4,
        out_specs=[VM] * 6,
        scratch_shapes=[
            pltpu.VMEM((KP, 2 * LC), bf16),
            pltpu.VMEM((DEPTH, PIECE, NS), f32),
            pltpu.SemaphoreType.DMA((DEPTH,)),
        ],
        compiler_params=params(20),
        cost_estimate=pl.CostEstimate(
            flops=8 * NS * KP * LC, bytes_accessed=4 * NS * NS, transcendentals=0
        ),
        name="split",
    )(near_source, position, slot, in_hbm(schur_block), pc, pg, blocks, act_wide)
    high, low = kept(high), kept(low)
    near_in = sent(near, 1, 0)

    relayed = [shape(NEAR + CAP + extra, LC) for extra in ((SEG, 0, G) if HOP == 2 else (SEG, G, 0))]
    outgoing = pl.pallas_call(
        relay_kernel,
        out_shape=relayed + [index(SLOTS)],
        in_specs=[VM, VM, ANY],
        out_specs=[VM] * 3 + [SM],
        scratch_shapes=[pltpu.SMEM((SEG, 128), f32), pltpu.SemaphoreType.DMA],
        compiler_params=params(6),
        name="relay",
    )(far_in, pg, partial)
    incoming = [near_in] + [moved(outgoing[o - 1], 0, o - HOP) for o in range(1, W)]

    outs = pl.pallas_call(
        first_kernel,
        out_shape=[far_block, seg_block, seg_block, face_block, seg_block]
        + [shape(NS, LC), shape(CR, LC), shape(CR, LC)]
        + [index(SLOTS), index(SEG), index(SLOTS), shape(8, LC)],
        in_specs=[SM] + [VM] * 10 + [SM, VM, VM],
        out_specs=[VM] * 8 + [SM] * 3 + [VM],
        scratch_shapes=[
            pltpu.VMEM((CR, LC), f32),
            pltpu.VMEM((CR, LC), f32),
            pltpu.VMEM((K_LEFT + K_WIDE, 2 * LC), bf16),
            pltpu.SMEM((W * 8 + SEG, 128), f32),
            pltpu.SemaphoreType.DMA((W + 1,)),
        ],
        compiler_params=params(12),
        name="first",
    )(me, *incoming, forth, project, pc, pg, partial, mask, far_source, high, low)
    far, replies = outs[0], outs[1:5]
    u0, projected0, actives, slots, route, inverse, sums0 = outs[5:]

    far_in = sent(far, 1, BACK_HOP)
    replies = [sent(replies[0], -1, 0)] + [moved(replies[o], 0, BACK_HOP - o) for o in range(1, W)]
    near_back, next_left = replies[0], replies[2]

    *outgoing, far, near = pl.pallas_call(
        exchange_kernel,
        out_shape=[seg_block, face_block, seg_block, far_block, seg_block],
        in_specs=[SM] * 3 + [VM] * 6 + [ANY],
        out_specs=[VM] * 5,
        compiler_params=params(12),
        name="exchange",
    )(route, inverse, near_source, far_in, *replies[1:], u0, mask, near_back)
    far_back = sent(far, -1, -BACK_HOP)
    incoming = [sent(near, 1, 0)] + [moved(outgoing[o - 1], 0, o - BACK_HOP) for o in range(1, W)]

    partial, term = pl.pallas_call(
        master_kernel,
        out_shape=[shape(NS, LC), shape(CR, LC)],
        in_specs=[SM] + [VM] * 9,
        out_specs=[VM] * 2,
        scratch_shapes=[pltpu.VMEM((CR, LC), f32), pltpu.VMEM((K_WIDE, 2 * LC), bf16)],
        compiler_params=params(12),
        cost_estimate=pl.CostEstimate(flops=8 * NS * K_WIDE * LC, bytes_accessed=MIB, transcendentals=0),
        name="master",
    )(slots, *incoming, projected0, actives, forth, high, low)

    u1, q_glue, q_contact, sums = pl.pallas_call(
        second_kernel,
        out_shape=[shape(NS, LC), shape(G, LC), shape(CR, LC), shape(8, LC)],
        in_specs=[SM] * 2 + [VM] * 11,
        out_specs=[VM] * 4,
        scratch_shapes=[pltpu.VMEM((K_NEAR, LC), f32), pltpu.VMEM((K_NEAR + K_PAD, 2 * LC), bf16)],
        compiler_params=params(12),
        name="second",
    )(me, place, near_back, far_back, next_left, incoming[2], u0, mask, partial, term, sums0, high, low)

    replied, sums = pl.pallas_call(
        reply_kernel,
        out_shape=[shape(CR + 8, LC), shape(8, LC)],
        in_specs=[SM] + [VM] * 3,
        out_specs=[VM] * 2,
        compiler_params=params(8),
        cost_estimate=pl.CostEstimate(flops=0, bytes_accessed=8 * MIB, transcendentals=0),
        name="reply",
    )(slots, project, u1, sums)
    replied = sent(replied, -1, -1)
    sums, token = total(sums)

    *outgoing, = pl.pallas_call(
        select_kernel,
        out_shape=[seg_block, seg_block, face_block, seg_block],
        in_specs=[VM] * 2 + [ANY],
        out_specs=[VM] * 4,
        scratch_shapes=[pltpu.SMEM((8, 128), f32), pltpu.SemaphoreType.DMA],
        compiler_params=params(6),
        name="select",
    )(replied, u1, token)
    fetched = [moved(outgoing[o], 0, 1 - o) for o in range(W)]

    mult_glue, mult_contact, res_glue, res_contact = pl.pallas_call(
        last_kernel,
        out_shape=[shape(G, LC), shape(CR, LC)] * 2,
        in_specs=[SM] * 2 + [VM] * 11,
        out_specs=[VM] * 4,
        compiler_params=params(24),
        name="last",
    )(me, position, *fetched, u1, q_glue, q_contact, pc, pg, mask, sums)
    contact = (1, 1, SEG, SD, LC)
    return (
        mult_glue[None, None],
        mult_contact.reshape(contact),
        res_glue[None, None],
        res_contact.reshape(contact),
    )


def solution(mesh):
    in_specs = (
        P("body", "sub", None, None),
        P("body", "sub", None, None, None),
        P("body", "sub", None, None),
        P("body", "sub", None, None, None),
        P("body", "sub", None, None),
        P("body", "sub", None),
        P("body", "sub", None, None),
    )
    out_specs = (
        P("body", "sub", None, None),
        P("body", "sub", None, None, None),
        P("body", "sub", None, None),
        P("body", "sub", None, None, None),
    )
    return jax.shard_map(
        per_device, mesh=mesh, in_specs=in_specs, out_specs=out_specs, check_vma=False
    )
```
